32 devices in a mesh: rep: 2 (over y), dev: 4 (over z), sub: 4 (over x, core).
Axes of the slice: x: 2, y: 2, z: 4, core: 2. Of those that a mesh axis runs over, the one named last changes fastest.
Arguments:
- tokens: bfloat16 [256, 3072], P(('rep', 'dev', 'sub')), parts along dimension 0, may hold values from -6 to 6
- queries: bfloat16 [256, 3072], P(('rep', 'dev', 'sub')), parts along dimension 0, may hold values from -12 to 12
- request_key_cache: bfloat16 [256, 128, 512], P(('rep', 'dev', 'sub')), parts along dimension 0, may hold values from -12 to 12
- request_value_cache: bfloat16 [256, 128, 512], P(('rep', 'dev', 'sub')), parts along dimension 0, may hold values from -6 to 6
- lengths: int32 [256], P(('rep', 'dev', 'sub')), parts along dimension 0, may hold values from 2 to 128, as said below
- norm_gain: bfloat16 [3072], replicated, may hold values from 0.5 to 1.5
- router_weight: bfloat16 [3072, 4], replicated, may hold values from -0.109375 to 0.109375
- routes: int32 [256, 2], P(('rep', 'dev')), parts along dimension 0, may hold values from 0 to 3, all different within a row; in each aligned block of 32 rows (0 to 31, 32 to 63, ...) at most 26 rows name the same one
- gate_weight: bfloat16 [3072, 32768], P(None, ('dev', 'sub')), may hold values from -0.109375 to 0.109375
- up_weight: bfloat16 [3072, 32768], P(None, ('dev', 'sub')), may hold values from -0.109375 to 0.109375
- down_weight: bfloat16 [32768, 3072], P('dev', 'sub'), may hold values from -0.0625 to 0.0625
Outputs:
- layer_output: bfloat16 [256, 3072], P(('rep', 'dev', 'sub')), parts along dimension 0
The draws below stay inside these ranges and needn't reach their ends.
There are 2 independent parts, one for each index of `rep`. The reference program is written for one: setup_inputs(seed, part) draws one part's arguments, and reference() takes and returns one part's arrays. A program takes and returns all parts, laid end to end along the dimension named above; an argument that names none is the same for every part. Nothing has to cross between parts.
Inputs may be any that keep to these rules, and one draw needn't show every extreme that they name: `routes`: in each aligned block of 32 rows no expert is named by more than 26 rows, and some block reaches 26. `lengths`: some request's length is 128.
All inputs are finite; a program needn't handle non-finite values.
Results may differ from the reference program's by a relative error of at most 0.0059.
Values may be sent and summed in bfloat16 or wider, within the bound.
No kernel may reach another device: no remote copies, remote signals or barrier semaphores. Data moves between devices by JAX's collectives and lax.ppermute only.
A program may use at most 128 MiB of HBM per device.

```python
import math
import jax
import jax.numpy as jnp
import numpy as np
from jax import lax

D = 3072
HEAD_SIZE = 128
QUERY_HEADS = 24
KEY_VALUE_HEADS = 4
FF = 8192
EXPERTS = 4
CACHE_POSITIONS = 128
DECODE_TOKENS = 128
BLOCK = 32
CAP = 26


def draw_queries(key, part):
    key = jax.random.fold_in(key, 7)
    sampled_inputs = jnp.clip(jax.random.normal(key, (DECODE_TOKENS, QUERY_HEADS * HEAD_SIZE), jnp.float32), -6.0, 6.0)
    return sampled_inputs.astype(jnp.bfloat16)


def draw_request_key_cache(key, part):
    key = jax.random.fold_in(key, 9)
    sampled_inputs = jnp.clip(jax.random.normal(key, (DECODE_TOKENS, CACHE_POSITIONS, KEY_VALUE_HEADS * HEAD_SIZE), jnp.float32), -6.0, 6.0)
    return sampled_inputs.astype(jnp.bfloat16)


def draw_lengths(key, part):
    key = jax.random.fold_in(key, 5)
    len_key, spot_key = jax.random.split(key)
    sampled_inputs = jax.random.randint(len_key, (DECODE_TOKENS,), 2, CACHE_POSITIONS + 1)
    spot = jax.random.randint(spot_key, (), 0, DECODE_TOKENS)
    return jnp.where(jnp.arange(DECODE_TOKENS) == spot, CACHE_POSITIONS, sampled_inputs).astype(jnp.int32)


def steps_of(stream_key, dims, cuts, least, top_value):
    def one(dim, parts):
        steps = jax.random.uniform(jax.random.fold_in(jax.random.fold_in(stream_key, 6), dim), (parts,), jnp.float32, least / len(cuts), top_value / len(cuts))
        return jnp.repeat(jnp.exp(steps), dims[dim] // parts).reshape((-1,) + (1,) * (len(dims) - dim - 1))

    gain = one(*cuts[0])
    for cut in cuts[1:]:
        gain = gain * one(*cut)
    return gain


def deal_out(rng, own, number, rows, count, top, limit, skew):
    ranking = jax.random.permutation(rng, count)
    packed, ordinary = portions_of(count, rows * top, limit, skew, True), portions_of(count, rows * top, limit, skew, False)
    places = jnp.arange(count)

    def named(tallies, rotation):
        used = int((tallies > 0).sum())
        fixed = max(1, used // 4)
        moved = fixed + (places - fixed + rotation * (used - fixed)) % max(1, count - fixed)
        return jnp.zeros((count,), jnp.int32).at[ranking[jnp.where(places < fixed, places, moved)]].set(jnp.asarray(tallies, jnp.int32))

    tallies = jnp.where(number % 4 == 0, named(packed, number // 4), named(ordinary, number - number // 4 - 1))
    mixed = jax.random.permutation(jax.random.fold_in(own, 3), count)
    source_of, receiver = mixed[0:count // 2 * 2:2], mixed[1:count // 2 * 2:2]
    room = jnp.minimum(tallies[source_of] - 1, limit - tallies[receiver]) // 2
    room = jnp.where((source_of == ranking[0]) | (receiver == ranking[0]) | (tallies[receiver] == 0), 0, jnp.maximum(room, 0))
    moved = jax.random.randint(jax.random.fold_in(own, 4), (count // 2,), 0, 1 << 20) % (room + 1)
    tallies = tallies.at[source_of].add(-moved).at[receiver].add(moved)
    labels = jnp.searchsorted(jnp.cumsum(tallies), jnp.arange(rows * top), side="right").astype(jnp.int32)
    table = labels.reshape(top, rows).T
    table = table[jax.random.permutation(jax.random.fold_in(own, 1), rows)]
    rotation = jax.random.randint(jax.random.fold_in(own, 2), (rows, 1), 0, top)
    return jnp.take_along_axis(table, (jnp.arange(top)[None, :] + rotation) % top, axis=1)


def portions_of(count, total, limit, slope, full):
    loads = [(1 << 20) // math.isqrt(grade ** slope) + 1 for grade in range(1, count + 1)]
    largest = limit if full else min(limit, max(-(-total // count), total * loads[0] // sum(loads)))
    least = 1 if total - largest >= count - 1 else 0
    holding, rest = [largest] + [least] * (count - 1), total - largest - least * (count - 1)
    while rest > 0:
        movable = [i for i in range(1, count) if holding[i] < largest] or [i for i in range(1, count) if holding[i] < limit]
        pool, budget = sum([loads[i] for i in movable]), rest
        for i in movable:
            addition = min(limit - holding[i], max(1, budget * loads[i] // pool), rest)
            holding[i] = holding[i] + addition
            rest = rest - addition
    return np.array(holding)


def scatter_about(own_key, shape, width, bound, cuts=(), kind=jnp.bfloat16):
    drawn = jax.random.normal(own_key, shape, jnp.float32) * width
    if len(cuts) > 0:
        drawn = steps_of(own_key, shape, cuts, -0.22, 0.18) * drawn
    return jnp.clip(drawn, min=-bound, max=bound).astype(kind)


def setup_inputs(seed: int = 0, part: int = 0) -> dict:
    keys = jax.random.split(jax.random.key(seed), 12)
    part_splits = jax.random.split(jax.random.fold_in(keys[11], part), 12)
    tokens = scatter_about(part_splits[0], (DECODE_TOKENS, D), 1.0, 6.0, ((0, 16),))
    queries = draw_queries(jax.random.fold_in(jax.random.fold_in(keys[11], part), 71), part)
    request_key_cache = draw_request_key_cache(jax.random.fold_in(jax.random.fold_in(keys[11], part), 71), part)
    request_value_cache = scatter_about(part_splits[3], (DECODE_TOKENS, CACHE_POSITIONS, KEY_VALUE_HEADS * HEAD_SIZE), 1.0, 6.0, ((0, 16),))
    lengths = draw_lengths(jax.random.fold_in(jax.random.fold_in(keys[11], part), 71), part)
    norm_gain = jnp.clip(1.0 + 0.1 * jax.random.normal(keys[5], (D,), jnp.float32), 0.5, 1.5).astype(jnp.bfloat16)
    router_weight = scatter_about(keys[6], (D, EXPERTS), D ** -0.5, 0.109375)
    routes_keys = jax.random.split(jax.random.fold_in(part_splits[7], 1), DECODE_TOKENS // BLOCK)
    routes_turns = jax.random.permutation(jax.random.fold_in(part_splits[7], 3), DECODE_TOKENS // BLOCK)
    routes = jax.vmap(lambda own, number: deal_out(jax.random.fold_in(part_splits[7], 2), own, number, BLOCK, EXPERTS, 2, CAP, 2))(routes_keys, routes_turns).reshape((DECODE_TOKENS, 2))
    gate_weight = scatter_about(keys[8], (D, EXPERTS * FF), D ** -0.5, 0.109375, ((1, 16),))
    up_weight = scatter_about(keys[9], (D, EXPERTS * FF), D ** -0.5, 0.109375, ((1, 16),))
    down_weight = scatter_about(keys[10], (EXPERTS * FF, D), FF ** -0.5, 0.0625, ((0, 4), (1, 4)))
    return dict(tokens=tokens, queries=queries, request_key_cache=request_key_cache, request_value_cache=request_value_cache, lengths=lengths, norm_gain=norm_gain, router_weight=router_weight, routes=routes, gate_weight=gate_weight, up_weight=up_weight, down_weight=down_weight)


def attend_one(single_query_row, cached_key_rows, cached_value_rows, live_count):
    device_group = QUERY_HEADS // KEY_VALUE_HEADS
    query_tensor_three = single_query_row.astype(jnp.float32).reshape(KEY_VALUE_HEADS, device_group, HEAD_SIZE)
    key_tensor_three = cached_key_rows.astype(jnp.float32).reshape(CACHE_POSITIONS, KEY_VALUE_HEADS, HEAD_SIZE)
    value_tensor_three = cached_value_rows.astype(jnp.float32).reshape(CACHE_POSITIONS, KEY_VALUE_HEADS, HEAD_SIZE)
    scores = jnp.einsum('hgd,chd->hgc', query_tensor_three, key_tensor_three) * (1.0 / math.sqrt(HEAD_SIZE))
    in_cache = jnp.arange(CACHE_POSITIONS) < live_count
    scores = jnp.where(in_cache[None, None, :], scores, -jnp.inf)
    peak_score = lax.optimization_barrier(jnp.max(scores, axis=-1, keepdims=True))
    exp_scores = jnp.exp(scores - peak_score)
    weights_bf = (exp_scores / lax.optimization_barrier(jnp.sum(exp_scores, axis=-1, keepdims=True))).astype(jnp.bfloat16)
    attended = jnp.einsum('hgc,chd->hgd', weights_bf.astype(jnp.float32), value_tensor_three)
    return attended.reshape(QUERY_HEADS * HEAD_SIZE)

def reference(tokens, queries, request_key_cache, request_value_cache, lengths, norm_gain, router_weight, routes, gate_weight, up_weight, down_weight):
    attended = lax.map(lambda pieces: attend_one(*pieces), (queries, request_key_cache, request_value_cache, lengths))
    resid = (tokens.astype(jnp.float32) + attended).astype(jnp.bfloat16)
    resid_f = resid.astype(jnp.float32)
    stats = lax.optimization_barrier(jnp.mean(resid_f * resid_f, axis=-1, keepdims=True))
    normed = (resid_f * lax.rsqrt(stats + 1e-05) * norm_gain.astype(jnp.float32)).astype(jnp.bfloat16)
    logits = jnp.dot(normed, router_weight, preferred_element_type=jnp.float32)
    expert_ids = jnp.arange(EXPERTS)
    first_logit = lax.optimization_barrier(jnp.sum(jnp.where(routes[:, 0:1] == expert_ids[None, :], logits, 0.0), axis=1))
    second_logit = lax.optimization_barrier(jnp.sum(jnp.where(routes[:, 1:2] == expert_ids[None, :], logits, 0.0), axis=1))
    first_share = jax.nn.sigmoid(first_logit - second_logit)
    second_share = jax.nn.sigmoid(second_logit - first_logit)
    mixture = jnp.zeros((DECODE_TOKENS, D), jnp.float32)
    for expert_num in range(EXPERTS):
        low = expert_num * FF
        gate_part = jnp.dot(normed, gate_weight[:, low:low + FF], preferred_element_type=jnp.float32)
        up_part = jnp.dot(normed, up_weight[:, low:low + FF], preferred_element_type=jnp.float32)
        hidden = (jax.nn.silu(gate_part) * up_part).astype(jnp.bfloat16)
        expert_y = jnp.dot(hidden, down_weight[low:low + FF, :], preferred_element_type=jnp.float32)
        share_now = jnp.where(routes[:, 0] == expert_num, first_share, 0.0) + jnp.where(routes[:, 1] == expert_num, second_share, 0.0)
        mixture = mixture + share_now[:, None] * expert_y
    return (resid_f + mixture).astype(jnp.bfloat16)
```

```python
import math

import jax
import jax.numpy as jnp
from jax import lax
from jax.experimental import pallas as pl
from jax.experimental.pallas import tpu as pltpu
from jax.sharding import PartitionSpec as P

HEAD_SIZE = 128
QUERY_HEADS = 24
KEY_VALUE_HEADS = 4
EXPERTS = 4


def general_plan(
    tokens,
    queries,
    request_key_cache,
    request_value_cache,
    lengths,
    norm_gain,
    router_weight,
    routes,
    gate_weight,
    up_weight,
    down_weight,
):
    token_count = tokens.shape[0]
    feat_width = tokens.shape[1]
    cache_length = request_key_cache.shape[1]
    device_group = QUERY_HEADS // KEY_VALUE_HEADS
    query_tensor_four = queries.reshape(token_count, KEY_VALUE_HEADS, device_group, HEAD_SIZE)
    key_tensor_four = request_key_cache.reshape(
        token_count, cache_length, KEY_VALUE_HEADS, HEAD_SIZE
    )
    value_tensor_four = request_value_cache.reshape(
        token_count, cache_length, KEY_VALUE_HEADS, HEAD_SIZE
    )
    scores = jnp.einsum(
        "thgd,tchd->thgc", query_tensor_four, key_tensor_four, preferred_element_type=jnp.float32
    ) * (1.0 / math.sqrt(HEAD_SIZE))
    in_cache = (jnp.arange(cache_length)[None, :] < lengths[:, None])[:, None, None, :]
    scores = jnp.where(in_cache, scores, -jnp.inf)
    peak_score = jnp.max(scores, axis=-1, keepdims=True)
    exp_scores = jnp.exp(scores - peak_score)
    weights_bf = (exp_scores / jnp.sum(exp_scores, axis=-1, keepdims=True)).astype(jnp.bfloat16)
    attended = jnp.einsum(
        "thgc,tchd->thgd", weights_bf, value_tensor_four, preferred_element_type=jnp.float32
    ).reshape(token_count, feat_width)
    resid = (tokens.astype(jnp.float32) + attended).astype(jnp.bfloat16)
    resid_f = resid.astype(jnp.float32)
    stats = jnp.mean(resid_f * resid_f, axis=-1, keepdims=True)
    normed = (resid_f * lax.rsqrt(stats + 1e-05) * norm_gain.astype(jnp.float32)).astype(
        jnp.bfloat16
    )
    logits = jnp.dot(normed, router_weight, preferred_element_type=jnp.float32)
    sub_index = lax.axis_index("sub")
    sub_count = lax.axis_size("sub")
    dev_count = lax.axis_size("dev")
    expert_ids = jnp.arange(EXPERTS)
    own_routes = lax.dynamic_slice_in_dim(routes, sub_index * token_count, token_count, 0)
    first_logit = jnp.sum(jnp.where(own_routes[:, 0:1] == expert_ids[None, :], logits, 0.0), axis=1)
    second_logit = jnp.sum(
        jnp.where(own_routes[:, 1:2] == expert_ids[None, :], logits, 0.0), axis=1
    )
    first_share = jax.nn.sigmoid(first_logit - second_logit)
    second_share = jax.nn.sigmoid(second_logit - first_logit)
    block_rows = lax.all_gather(normed, "sub", axis=0, tiled=True)
    block_len = token_count * sub_count
    capacity = 5 * block_len // 6
    group_size = dev_count // EXPERTS
    flat_ids = routes.reshape(-1)
    route_hot = (flat_ids[:, None] == expert_ids[None, :]).astype(jnp.int32)
    earlier = jnp.cumsum(route_hot, axis=0) - route_hot
    slot_number = jnp.sum(earlier * route_hot, axis=1)
    slot_index = (flat_ids * capacity + slot_number).reshape(block_len, 2)
    slot_range = jnp.arange(EXPERTS * capacity)
    place_matrix = jnp.any(slot_index[None, :, :] == slot_range[:, None, None], axis=-1).astype(
        jnp.bfloat16
    )
    slot_total = dev_count * capacity
    packed = jnp.dot(place_matrix, block_rows, preferred_element_type=jnp.float32).astype(
        jnp.bfloat16
    )
    outgoing = jnp.repeat(packed.reshape(EXPERTS, capacity, feat_width), group_size, axis=0)
    arrived = lax.all_to_all(outgoing, "dev", split_axis=0, concat_axis=0, tiled=True).reshape(
        slot_total, feat_width
    )
    gate_part = jnp.dot(arrived, gate_weight, preferred_element_type=jnp.float32)
    up_part = jnp.dot(arrived, up_weight, preferred_element_type=jnp.float32)
    hidden = (jax.nn.silu(gate_part) * up_part).astype(jnp.bfloat16)
    out_width = down_weight.shape[1]
    partial_out = jnp.dot(
        lax.all_gather(hidden, "sub", axis=1, tiled=True),
        down_weight,
        preferred_element_type=jnp.float32,
    )
    returned = lax.all_to_all(
        partial_out.reshape(dev_count, capacity, out_width),
        "dev",
        split_axis=0,
        concat_axis=0,
        tiled=True,
    )
    expert_out = jnp.sum(
        returned.reshape(EXPERTS, group_size, capacity, out_width), axis=1
    ).reshape(EXPERTS * capacity, out_width)
    pick_matrix = (slot_index.reshape(-1)[:, None] == slot_range[None, :]).astype(jnp.float32)
    per_route = jnp.dot(pick_matrix, expert_out, precision=lax.Precision.HIGHEST).reshape(
        block_len, 2, out_width
    )
    own_outputs = lax.all_to_all(per_route, "sub", split_axis=0, concat_axis=2, tiled=True)
    mixture = (
        first_share[:, None] * own_outputs[:, 0, :] + second_share[:, None] * own_outputs[:, 1, :]
    )
    return (resid_f + mixture).astype(jnp.bfloat16)


VMEM_SPEC = pl.BlockSpec(memory_space=pltpu.VMEM)
SMEM_SPEC = pl.BlockSpec(memory_space=pltpu.SMEM)
MIB = 1024 * 1024
EXTRA = 128


def call(body, out_shapes, operands, specs, flops, vmem, scratch=(), bytes_accessed=0):
    return pl.pallas_call(
        body,
        out_shape=out_shapes,
        in_specs=specs,
        out_specs=jax.tree.map(lambda _: VMEM_SPEC, out_shapes),
        scratch_shapes=list(scratch),
        compiler_params=pltpu.CompilerParams(vmem_limit_bytes=vmem),
        cost_estimate=pl.CostEstimate(
            flops=flops, bytes_accessed=bytes_accessed, transcendentals=0
        ),
    )(*operands)


def dot(a, b):
    return jnp.dot(a, b, preferred_element_type=jnp.float32)


def dot_nt(a, b):
    return lax.dot_general(a, b, (((1,), (1,)), ((), ())), preferred_element_type=jnp.float32)


def attention_kernel(
    lengths_ref,
    routes_ref,
    tokens_ref,
    queries_ref,
    keys_ref,
    values_ref,
    gain_ref,
    router_ref,
    payload_ref,
    resid_ref,
    att_ref,
):
    rows, width = tokens_ref.shape
    cache = keys_ref.shape[1]
    group = QUERY_HEADS // KEY_VALUE_HEADS
    row = lax.broadcasted_iota(jnp.int32, (rows, 1), 0)
    live = jnp.zeros((rows, 1), jnp.int32)
    first = jnp.zeros((rows, 1), jnp.int32)
    second = jnp.zeros((rows, 1), jnp.int32)
    base = lax.axis_index("sub") * rows
    for t in range(rows):
        live = jnp.where(row == t, lengths_ref[t], live)
        first = jnp.where(row == t, routes_ref[0, base + t], first)
        second = jnp.where(row == t, routes_ref[1, base + t], second)
    column = lax.broadcasted_iota(jnp.int32, (rows, rows * cache), 1)
    start = row * cache
    in_cache = (column >= start) & (column < start + live)
    in_cache = jnp.concatenate([in_cache.astype(jnp.int32)] * group, axis=0) > 0
    scale = 1.0 / math.sqrt(HEAD_SIZE)
    for kv in range(KEY_VALUE_HEADS):
        heads = [queries_ref[:, h * HEAD_SIZE : (h + 1) * HEAD_SIZE].astype(jnp.float32)
                 for h in range(kv * group, (kv + 1) * group)]
        query = jnp.concatenate(heads, axis=0).astype(jnp.bfloat16)
        lanes = slice(kv * HEAD_SIZE, (kv + 1) * HEAD_SIZE)
        key = keys_ref[:, :, lanes].reshape(rows * cache, HEAD_SIZE)
        value = values_ref[:, :, lanes].reshape(rows * cache, HEAD_SIZE)
        scores = jnp.where(in_cache, dot_nt(query, key) * scale, -jnp.inf)
        exp_scores = jnp.exp(scores - jnp.max(scores, axis=1, keepdims=True))
        total = jnp.sum(exp_scores, axis=1, keepdims=True)
        probs = (exp_scores * (1.0 / total)).astype(jnp.bfloat16)
        attended = dot(probs, value)
        for g in range(group):
            h = kv * group + g
            att_ref[:, h * HEAD_SIZE : (h + 1) * HEAD_SIZE] = attended[g * rows : (g + 1) * rows]
    resid = (tokens_ref[...].astype(jnp.float32) + att_ref[...]).astype(jnp.bfloat16)
    resid_ref[...] = resid
    resid_f = resid.astype(jnp.float32)
    stats = jnp.sum(resid_f * resid_f, axis=1, keepdims=True) * (1.0 / width)
    gain = gain_ref[...].astype(jnp.float32).reshape(1, width)
    normed = (resid_f * lax.rsqrt(stats + 1e-05) * gain).astype(jnp.bfloat16)
    payload_ref[:, :width] = normed
    logits = dot_nt(normed, router_ref[...])
    expert = lax.broadcasted_iota(jnp.int32, (rows, EXPERTS), 1)
    first_logit = jnp.sum(jnp.where(first == expert, logits, 0.0), axis=1, keepdims=True)
    second_logit = jnp.sum(jnp.where(second == expert, logits, 0.0), axis=1, keepdims=True)
    first_share = 1.0 / (1.0 + jnp.exp(second_logit - first_logit))
    second_share = 1.0 / (1.0 + jnp.exp(first_logit - second_logit))
    lane = lax.broadcasted_iota(jnp.int32, (rows, EXTRA), 1)
    place = lane % EXPERTS
    routed = ((first == place) | (second == place)).astype(jnp.float32)
    share = jnp.where(first == place, first_share, 0.0) + jnp.where(second == place, second_share, 0.0)
    high = share.astype(jnp.bfloat16).astype(jnp.float32)
    low = share - high
    extra = jnp.where(
        lane < EXPERTS,
        routed,
        jnp.where(lane < 2 * EXPERTS, high, jnp.where(lane < 3 * EXPERTS, low, 0.0)),
    )
    payload_ref[:, width:] = extra.astype(jnp.bfloat16)


def own_offset(rows):
    return (lax.axis_index("dev") * lax.axis_size("sub") + lax.axis_index("sub")) * rows


def slot_matrix(extra, offset):
    count = extra.shape[0]
    here = lax.broadcasted_iota(jnp.int32, (count, count), 0) ^ offset
    there = lax.broadcasted_iota(jnp.int32, (count, count), 1) ^ offset
    earlier = dot((there < here).astype(jnp.bfloat16), extra)
    lane = lax.broadcasted_iota(jnp.int32, (count, EXTRA), 1)
    mine = lane == lax.axis_index("dev")
    rank = jnp.sum(jnp.where(mine, earlier, 0.0), axis=1, keepdims=True)
    routed = jnp.sum(jnp.where(mine, extra.astype(jnp.float32), 0.0), axis=1, keepdims=True)
    slot = jnp.where(routed > 0.5, rank, -1.0).astype(jnp.int32)
    return (slot == lax.broadcasted_iota(jnp.int32, (count, count), 1)).astype(jnp.float32)


def hidden_columns(x, gate_ref, up_ref, out_ref, begin):
    step = 256
    for j in range(0, out_ref.shape[1], step):
        gate = dot(x, gate_ref[:, begin + j : begin + j + step])
        up = dot(x, up_ref[:, begin + j : begin + j + step])
        out_ref[:, j : j + step] = (gate / (1.0 + jnp.exp(-gate)) * up).astype(jnp.bfloat16)


def first_hidden_kernel(pieces, slots, *refs):
    piece_refs = refs[:pieces]
    gate_ref, up_ref, x_ref, extra_ref, hidden_ref, rows_ref = refs[pieces:]
    width = x_ref.shape[1]
    at = 0
    for first, second in zip(piece_refs[0::2], piece_refs[1::2], strict=True):
        both = [first[...].astype(jnp.float32), second[...].astype(jnp.float32)]
        size = first.shape[0] + second.shape[0]
        rows_ref[at : at + size, :] = jnp.concatenate(both, axis=0).astype(jnp.bfloat16)
        at += size
    extra = rows_ref[:, width:]
    extra_ref[...] = extra
    rows = piece_refs[0].shape[0]
    place = slot_matrix(extra, own_offset(rows)).T[:slots].astype(jnp.bfloat16)
    x_ref[...] = dot(place, rows_ref[:, :width]).astype(jnp.bfloat16)
    hidden_columns(x_ref[...], gate_ref, up_ref, hidden_ref, 0)


def next_hidden_kernel(begin, x_ref, gate_ref, up_ref, hidden_ref):
    hidden_columns(x_ref[...], gate_ref, up_ref, hidden_ref, begin)


def down_part(sources, down_ref, own_width):
    sub = lax.axis_index("sub")
    total = None
    for hidden_ref, flip, begin in sources:
        height = hidden_ref.shape[1]
        at = pl.multiple_of((sub ^ flip) * own_width + begin, 256)
        part = dot(hidden_ref[...], down_ref[pl.ds(at, height), :])
        total = part if total is None else total + part
    return total


def down_kernel(flips, own_width, has_total, *refs):
    count = len(flips)
    hidden_refs = refs[:count]
    rest = refs[count:]
    sources = [(r, f, b) for r, (f, b) in zip(hidden_refs, flips, strict=True)]
    total = down_part(sources, rest[0], own_width)
    if has_total:
        total = total + rest[1][...]
    rest[-1][...] = total


def last_down_kernel(flips, own_width, rows, *refs):
    count = len(flips)
    hidden_refs = refs[:count]
    down_ref, total_ref, extra_ref, out_ref = refs[count:]
    sources = [(r, f, b) for r, (f, b) in zip(hidden_refs, flips, strict=True)]
    slots = total_ref.shape[0]
    offset = own_offset(rows)
    extra = extra_ref[...]
    tokens = extra.shape[0]
    here = slot_matrix(extra, offset)
    lane = lax.broadcasted_iota(jnp.int32, (tokens, EXTRA), 1)
    dev = lax.axis_index("dev")
    mine = (lane == EXPERTS + dev) | (lane == 2 * EXPERTS + dev)
    shares = jnp.where(mine, extra.astype(jnp.float32), 0.0).astype(jnp.bfloat16)
    by_slot = dot(here.T[:slots].astype(jnp.bfloat16), shares)
    share = jnp.sum(by_slot, axis=1, keepdims=True)
    token = lax.broadcasted_iota(jnp.int32, (tokens, tokens), 0)
    moved = (token ^ offset) == lax.broadcasted_iota(jnp.int32, (tokens, tokens), 1)
    spread = dot(moved.astype(jnp.bfloat16), here.astype(jnp.bfloat16)).astype(jnp.bfloat16)
    total = total_ref[...] + down_part(sources, down_ref, own_width)
    out_ref[...] = dot(spread[:, :slots], (total * share).astype(jnp.bfloat16)).astype(jnp.bfloat16)


def finish_kernel(resid_ref, arrived_ref, out_ref):
    subs, devs = lax.axis_size("sub"), lax.axis_size("dev")
    width = arrived_ref.shape[2]
    for s in range(subs):
        lanes = slice(s * width, (s + 1) * width)
        mixture = arrived_ref[s].astype(jnp.float32)
        for d in range(1, devs):
            mixture = mixture + arrived_ref[d * subs + s].astype(jnp.float32)
        out_ref[:, lanes] = (resid_ref[:, lanes].astype(jnp.float32) + mixture).astype(jnp.bfloat16)


def flip(x, axis, bits):
    return lax.ppermute(x, axis, [(i, i ^ bits) for i in range(lax.axis_size(axis))])


def per_device(
    tokens,
    queries,
    request_key_cache,
    request_value_cache,
    lengths,
    norm_gain,
    router_weight,
    routes,
    gate_weight,
    up_weight,
    down_weight,
):
    rows, width = tokens.shape
    devs, subs = lax.axis_size("dev"), lax.axis_size("sub")
    all_rows = rows * devs * subs
    slots = devs * (5 * rows * subs // 6)
    own_hidden = gate_weight.shape[1]
    out_width = down_weight.shape[1]
    bf16 = jnp.bfloat16
    payload, resid = call(
        attention_kernel,
        (
            jax.ShapeDtypeStruct((rows, width + EXTRA), bf16),
            jax.ShapeDtypeStruct((rows, width), bf16),
        ),
        (
            lengths,
            routes.T,
            tokens,
            queries,
            request_key_cache,
            request_value_cache,
            norm_gain,
            router_weight.T,
        ),
        [SMEM_SPEC, SMEM_SPEC] + [VMEM_SPEC] * 6,
        flops=30 * 10**9,
        bytes_accessed=100 * MIB,
        vmem=8 * MIB,
        scratch=[pltpu.VMEM((rows, width), jnp.float32)],
    )
    over_z = [payload] + [flip(payload, "dev", k) for k in (1, 2, 3)]
    over_x = [flip(p, "sub", 2) for p in over_z]
    over_core = [[flip(p, "sub", 1) for p in group] for group in (over_z, over_x)]
    pieces = []
    for k in range(devs):
        pieces += [over_z[k], over_core[0][k], over_x[k], over_core[1][k]]
    half = own_hidden // 2
    x, extra, hidden_a = call(
        lambda *refs: first_hidden_kernel(len(pieces), slots, *refs),
        (
            jax.ShapeDtypeStruct((slots, width), bf16),
            jax.ShapeDtypeStruct((all_rows, EXTRA), bf16),
            jax.ShapeDtypeStruct((slots, half), bf16),
        ),
        (*pieces, gate_weight, up_weight),
        [VMEM_SPEC] * (len(pieces) + 2),
        flops=2 * 10**9,
        vmem=6 * MIB,
        scratch=[pltpu.VMEM((all_rows, width + EXTRA), bf16)],
    )
    hidden_b = call(
        lambda *refs: next_hidden_kernel(half, *refs),
        jax.ShapeDtypeStruct((slots, own_hidden - half), bf16),
        (x, gate_weight, up_weight),
        [VMEM_SPEC] * 3,
        flops=2 * 10**9,
        vmem=4 * MIB,
    )
    far_a, near_a = flip(hidden_a, "sub", 2), flip(hidden_a, "sub", 1)
    far_b, near_b = flip(hidden_b, "sub", 2), flip(hidden_b, "sub", 1)
    across_a, across_b = flip(far_a, "sub", 1), flip(far_b, "sub", 1)
    total_shape = jax.ShapeDtypeStruct((slots, out_width), jnp.float32)
    flips = ((0, 0), (0, half), (1, 0), (1, half))
    total = call(
        lambda *refs: down_kernel(flips, own_hidden, False, *refs),
        total_shape,
        (hidden_a, hidden_b, near_a, near_b, down_weight),
        [VMEM_SPEC] * 5,
        flops=10**9,
        vmem=4 * MIB,
    )
    flips_a = ((2, 0), (3, 0))
    total = call(
        lambda *refs: down_kernel(flips_a, own_hidden, True, *refs),
        total_shape,
        (far_a, across_a, down_weight, total),
        [VMEM_SPEC] * 4,
        flops=10**9,
        vmem=4 * MIB,
    )
    flips_b = ((2, half), (3, half))
    weighted = call(
        lambda *refs: last_down_kernel(flips_b, own_hidden, rows, *refs),
        jax.ShapeDtypeStruct((all_rows, out_width), bf16),
        (far_b, across_b, down_weight, total, extra),
        [VMEM_SPEC] * 5,
        flops=10**9,
        vmem=4 * MIB,
    )
    arrived = lax.all_to_all(
        weighted.reshape(devs * subs, rows, out_width),
        ("dev", "sub"),
        split_axis=0,
        concat_axis=0,
        tiled=True,
    )
    return call(
        finish_kernel,
        jax.ShapeDtypeStruct((rows, width), bf16),
        (resid, arrived),
        [VMEM_SPEC] * 2,
        flops=10**6,
        vmem=4 * MIB,
    )


def solution(mesh):
    in_specs = (
        P(("rep", "dev", "sub"), None),
        P(("rep", "dev", "sub"), None),
        P(("rep", "dev", "sub"), None, None),
        P(("rep", "dev", "sub"), None, None),
        P(("rep", "dev", "sub")),
        P(),
        P(),
        P(("rep", "dev"), None),
        P(None, ("dev", "sub")),
        P(None, ("dev", "sub")),
        P("dev", "sub"),
    )
    out_specs = P(("rep", "dev", "sub"), None)
    one_expert_each = mesh.shape["dev"] == EXPERTS and mesh.shape["sub"] == 4
    return jax.shard_map(
        per_device if one_expert_each else general_plan,
        mesh=mesh,
        in_specs=in_specs,
        out_specs=out_specs,
        check_vma=False,
    )
```

```python
import math

import jax
import jax.numpy as jnp
from jax import lax
from jax.experimental import pallas as pl
from jax.experimental.pallas import tpu as pltpu
from jax.sharding import PartitionSpec as P

HEAD_SIZE = 128
QUERY_HEADS = 24
KEY_VALUE_HEADS = 4
EXPERTS = 4


def general_plan(
    tokens,
    queries,
    request_key_cache,
    request_value_cache,
    lengths,
    norm_gain,
    router_weight,
    routes,
    gate_weight,
    up_weight,
    down_weight,
):
    token_count = tokens.shape[0]
    feat_width = tokens.shape[1]
    cache_length = request_key_cache.shape[1]
    device_group = QUERY_HEADS // KEY_VALUE_HEADS
    query_tensor_four = queries.reshape(token_count, KEY_VALUE_HEADS, device_group, HEAD_SIZE)
    key_tensor_four = request_key_cache.reshape(
        token_count, cache_length, KEY_VALUE_HEADS, HEAD_SIZE
    )
    value_tensor_four = request_value_cache.reshape(
        token_count, cache_length, KEY_VALUE_HEADS, HEAD_SIZE
    )
    scores = jnp.einsum(
        "thgd,tchd->thgc", query_tensor_four, key_tensor_four, preferred_element_type=jnp.float32
    ) * (1.0 / math.sqrt(HEAD_SIZE))
    in_cache = (jnp.arange(cache_length)[None, :] < lengths[:, None])[:, None, None, :]
    scores = jnp.where(in_cache, scores, -jnp.inf)
    peak_score = jnp.max(scores, axis=-1, keepdims=True)
    exp_scores = jnp.exp(scores - peak_score)
    weights_bf = (exp_scores / jnp.sum(exp_scores, axis=-1, keepdims=True)).astype(jnp.bfloat16)
    attended = jnp.einsum(
        "thgc,tchd->thgd", weights_bf, value_tensor_four, preferred_element_type=jnp.float32
    ).reshape(token_count, feat_width)
    resid = (tokens.astype(jnp.float32) + attended).astype(jnp.bfloat16)
    resid_f = resid.astype(jnp.float32)
    stats = jnp.mean(resid_f * resid_f, axis=-1, keepdims=True)
    normed = (resid_f * lax.rsqrt(stats + 1e-05) * norm_gain.astype(jnp.float32)).astype(
        jnp.bfloat16
    )
    logits = jnp.dot(normed, router_weight, preferred_element_type=jnp.float32)
    sub_index = lax.axis_index("sub")
    sub_count = lax.axis_size("sub")
    dev_count = lax.axis_size("dev")
    expert_ids = jnp.arange(EXPERTS)
    own_routes = lax.dynamic_slice_in_dim(routes, sub_index * token_count, token_count, 0)
    first_logit = jnp.sum(jnp.where(own_routes[:, 0:1] == expert_ids[None, :], logits, 0.0), axis=1)
    second_logit = jnp.sum(
        jnp.where(own_routes[:, 1:2] == expert_ids[None, :], logits, 0.0), axis=1
    )
    first_share = jax.nn.sigmoid(first_logit - second_logit)
    second_share = jax.nn.sigmoid(second_logit - first_logit)
    block_rows = lax.all_gather(normed, "sub", axis=0, tiled=True)
    block_len = token_count * sub_count
    capacity = 5 * block_len // 6
    group_size = dev_count // EXPERTS
    flat_ids = routes.reshape(-1)
    route_hot = (flat_ids[:, None] == expert_ids[None, :]).astype(jnp.int32)
    earlier = jnp.cumsum(route_hot, axis=0) - route_hot
    slot_number = jnp.sum(earlier * route_hot, axis=1)
    slot_index = (flat_ids * capacity + slot_number).reshape(block_len, 2)
    slot_range = jnp.arange(EXPERTS * capacity)
    place_matrix = jnp.any(slot_index[None, :, :] == slot_range[:, None, None], axis=-1).astype(
        jnp.bfloat16
    )
    slot_total = dev_count * capacity
    packed = jnp.dot(place_matrix, block_rows, preferred_element_type=jnp.float32).astype(
        jnp.bfloat16
    )
    outgoing = jnp.repeat(packed.reshape(EXPERTS, capacity, feat_width), group_size, axis=0)
    arrived = lax.all_to_all(outgoing, "dev", split_axis=0, concat_axis=0, tiled=True).reshape(
        slot_total, feat_width
    )
    gate_part = jnp.dot(arrived, gate_weight, preferred_element_type=jnp.float32)
    up_part = jnp.dot(arrived, up_weight, preferred_element_type=jnp.float32)
    hidden = (jax.nn.silu(gate_part) * up_part).astype(jnp.bfloat16)
    out_width = down_weight.shape[1]
    partial_out = jnp.dot(
        lax.all_gather(hidden, "sub", axis=1, tiled=True),
        down_weight,
        preferred_element_type=jnp.float32,
    )
    returned = lax.all_to_all(
        partial_out.reshape(dev_count, capacity, out_width),
        "dev",
        split_axis=0,
        concat_axis=0,
        tiled=True,
    )
    expert_out = jnp.sum(
        returned.reshape(EXPERTS, group_size, capacity, out_width), axis=1
    ).reshape(EXPERTS * capacity, out_width)
    pick_matrix = (slot_index.reshape(-1)[:, None] == slot_range[None, :]).astype(jnp.float32)
    per_route = jnp.dot(pick_matrix, expert_out, precision=lax.Precision.HIGHEST).reshape(
        block_len, 2, out_width
    )
    own_outputs = lax.all_to_all(per_route, "sub", split_axis=0, concat_axis=2, tiled=True)
    mixture = (
        first_share[:, None] * own_outputs[:, 0, :] + second_share[:, None] * own_outputs[:, 1, :]
    )
    return (resid_f + mixture).astype(jnp.bfloat16)


VMEM_SPEC = pl.BlockSpec(memory_space=pltpu.VMEM)
SMEM_SPEC = pl.BlockSpec(memory_space=pltpu.SMEM)
MIB = 1024 * 1024
OPENING_FLOPS = 4 * 10**9
EXTRA = 128


def call(body, out_shapes, operands, specs, flops, vmem, scratch=(), bytes_accessed=0):
    return pl.pallas_call(
        body,
        out_shape=out_shapes,
        in_specs=specs,
        out_specs=jax.tree.map(lambda _: VMEM_SPEC, out_shapes),
        scratch_shapes=list(scratch),
        compiler_params=pltpu.CompilerParams(vmem_limit_bytes=vmem),
        cost_estimate=pl.CostEstimate(
            flops=flops, bytes_accessed=bytes_accessed, transcendentals=0
        ),
    )(*operands)


def dot(a, b):
    return jnp.dot(a, b, preferred_element_type=jnp.float32)


def dot_nt(a, b):
    return lax.dot_general(a, b, (((1,), (1,)), ((), ())), preferred_element_type=jnp.float32)


def opening_kernel(out_ref):
    out_ref[...] = jnp.zeros_like(out_ref)


def attention_kernel(
    _,
    lengths_ref,
    routes_ref,
    queries_ref,
    keys_ref,
    values_ref,
    tokens_ref,
    gain_ref,
    router_ref,
    payload_ref,
    resid_ref,
    att_ref,
):
    rows, width = tokens_ref.shape
    cache = keys_ref.shape[1]
    group = QUERY_HEADS // KEY_VALUE_HEADS
    row = lax.broadcasted_iota(jnp.int32, (rows, 1), 0)
    live = jnp.zeros((rows, 1), jnp.int32)
    first = jnp.zeros((rows, 1), jnp.int32)
    second = jnp.zeros((rows, 1), jnp.int32)
    base = lax.axis_index("sub") * rows
    for t in range(rows):
        live = jnp.where(row == t, lengths_ref[t], live)
        first = jnp.where(row == t, routes_ref[0, base + t], first)
        second = jnp.where(row == t, routes_ref[1, base + t], second)
    column = lax.broadcasted_iota(jnp.int32, (rows, rows * cache), 1)
    start = row * cache
    in_cache = (column >= start) & (column < start + live)
    in_cache = jnp.concatenate([in_cache.astype(jnp.int32)] * group, axis=0) > 0
    scale = 1.0 / math.sqrt(HEAD_SIZE)
    for kv in range(KEY_VALUE_HEADS):
        heads = [queries_ref[:, h * HEAD_SIZE : (h + 1) * HEAD_SIZE].astype(jnp.float32)
                 for h in range(kv * group, (kv + 1) * group)]
        query = jnp.concatenate(heads, axis=0).astype(jnp.bfloat16)
        lanes = slice(kv * HEAD_SIZE, (kv + 1) * HEAD_SIZE)
        key = keys_ref[:, :, lanes].reshape(rows * cache, HEAD_SIZE)
        value = values_ref[:, :, lanes].reshape(rows * cache, HEAD_SIZE)
        scores = jnp.where(in_cache, dot_nt(query, key) * scale, -jnp.inf)
        exp_scores = jnp.exp(scores - jnp.max(scores, axis=1, keepdims=True))
        total = jnp.sum(exp_scores, axis=1, keepdims=True)
        probs = (exp_scores * (1.0 / total)).astype(jnp.bfloat16)
        attended = dot(probs, value)
        for g in range(group):
            h = kv * group + g
            att_ref[:, h * HEAD_SIZE : (h + 1) * HEAD_SIZE] = attended[g * rows : (g + 1) * rows]
    resid = (tokens_ref[...].astype(jnp.float32) + att_ref[...]).astype(jnp.bfloat16)
    resid_ref[...] = resid
    resid_f = resid.astype(jnp.float32)
    stats = jnp.sum(resid_f * resid_f, axis=1, keepdims=True) * (1.0 / width)
    gain = gain_ref[...].astype(jnp.float32).reshape(1, width)
    normed = (resid_f * lax.rsqrt(stats + 1e-05) * gain).astype(jnp.bfloat16)
    payload_ref[:, :width] = normed
    logits = dot_nt(normed, router_ref[...])
    expert = lax.broadcasted_iota(jnp.int32, (rows, EXPERTS), 1)
    first_logit = jnp.sum(jnp.where(first == expert, logits, 0.0), axis=1, keepdims=True)
    second_logit = jnp.sum(jnp.where(second == expert, logits, 0.0), axis=1, keepdims=True)
    first_share = 1.0 / (1.0 + jnp.exp(second_logit - first_logit))
    second_share = 1.0 / (1.0 + jnp.exp(first_logit - second_logit))
    lane = lax.broadcasted_iota(jnp.int32, (rows, EXTRA), 1)
    place = lane % EXPERTS
    routed = ((first == place) | (second == place)).astype(jnp.float32)
    share = jnp.where(first == place, first_share, 0.0) + jnp.where(second == place, second_share, 0.0)
    high = share.astype(jnp.bfloat16).astype(jnp.float32)
    low = share - high
    extra = jnp.where(
        lane < EXPERTS,
        routed,
        jnp.where(lane < 2 * EXPERTS, high, jnp.where(lane < 3 * EXPERTS, low, 0.0)),
    )
    payload_ref[:, width:] = extra.astype(jnp.bfloat16)


def own_offset(rows):
    return (lax.axis_index("dev") * lax.axis_size("sub") + lax.axis_index("sub")) * rows


def slot_matrix(extra, offset):
    count = extra.shape[0]
    here = lax.broadcasted_iota(jnp.int32, (count, count), 0) ^ offset
    there = lax.broadcasted_iota(jnp.int32, (count, count), 1) ^ offset
    earlier = dot((there < here).astype(jnp.bfloat16), extra)
    lane = lax.broadcasted_iota(jnp.int32, (count, EXTRA), 1)
    mine = lane == lax.axis_index("dev")
    rank = jnp.sum(jnp.where(mine, earlier, 0.0), axis=1, keepdims=True)
    routed = jnp.sum(jnp.where(mine, extra.astype(jnp.float32), 0.0), axis=1, keepdims=True)
    slot = jnp.where(routed > 0.5, rank, -1.0).astype(jnp.int32)
    return (slot == lax.broadcasted_iota(jnp.int32, (count, count), 1)).astype(jnp.float32)


def hidden_columns(x, gate_ref, up_ref, out_ref, begin):
    step = 256
    for j in range(0, out_ref.shape[1], step):
        gate = dot(x, gate_ref[:, begin + j : begin + j + step])
        up = dot(x, up_ref[:, begin + j : begin + j + step])
        out_ref[:, j : j + step] = (gate / (1.0 + jnp.exp(-gate)) * up).astype(jnp.bfloat16)


def first_hidden_kernel(pieces, slots, *refs):
    piece_refs = refs[:pieces]
    gate_ref, up_ref, x_ref, extra_ref, hidden_ref, rows_ref = refs[pieces:]
    width = x_ref.shape[1]
    at = 0
    for first, second in zip(piece_refs[0::2], piece_refs[1::2], strict=True):
        both = [first[...].astype(jnp.float32), second[...].astype(jnp.float32)]
        size = first.shape[0] + second.shape[0]
        rows_ref[at : at + size, :] = jnp.concatenate(both, axis=0).astype(jnp.bfloat16)
        at += size
    extra = rows_ref[:, width:]
    extra_ref[...] = extra
    rows = piece_refs[0].shape[0]
    place = slot_matrix(extra, own_offset(rows)).T[:slots].astype(jnp.bfloat16)
    x_ref[...] = dot(place, rows_ref[:, :width]).astype(jnp.bfloat16)
    hidden_columns(x_ref[...], gate_ref, up_ref, hidden_ref, 0)


def next_hidden_kernel(begin, x_ref, gate_ref, up_ref, hidden_ref):
    hidden_columns(x_ref[...], gate_ref, up_ref, hidden_ref, begin)


def down_part(sources, down_ref, own_width):
    sub = lax.axis_index("sub")
    total = None
    for hidden_ref, flip, begin in sources:
        height = hidden_ref.shape[1]
        at = pl.multiple_of((sub ^ flip) * own_width + begin, 256)
        part = dot(hidden_ref[...], down_ref[pl.ds(at, height), :])
        total = part if total is None else total + part
    return total


def down_kernel(flips, own_width, has_total, *refs):
    count = len(flips)
    hidden_refs = refs[:count]
    rest = refs[count:]
    sources = [(r, f, b) for r, (f, b) in zip(hidden_refs, flips, strict=True)]
    total = down_part(sources, rest[0], own_width)
    if has_total:
        total = total + rest[1][...]
    rest[-1][...] = total


def last_down_kernel(flips, own_width, rows, *refs):
    count = len(flips)
    hidden_refs = refs[:count]
    down_ref, total_ref, extra_ref, out_ref = refs[count:]
    sources = [(r, f, b) for r, (f, b) in zip(hidden_refs, flips, strict=True)]
    slots = total_ref.shape[0]
    offset = own_offset(rows)
    extra = extra_ref[...]
    tokens = extra.shape[0]
    here = slot_matrix(extra, offset)
    lane = lax.broadcasted_iota(jnp.int32, (tokens, EXTRA), 1)
    dev = lax.axis_index("dev")
    mine = (lane == EXPERTS + dev) | (lane == 2 * EXPERTS + dev)
    shares = jnp.where(mine, extra.astype(jnp.float32), 0.0).astype(jnp.bfloat16)
    by_slot = dot(here.T[:slots].astype(jnp.bfloat16), shares)
    share = jnp.sum(by_slot, axis=1, keepdims=True)
    token = lax.broadcasted_iota(jnp.int32, (tokens, tokens), 0)
    moved = (token ^ offset) == lax.broadcasted_iota(jnp.int32, (tokens, tokens), 1)
    spread = dot(moved.astype(jnp.bfloat16), here.astype(jnp.bfloat16)).astype(jnp.bfloat16)
    total = total_ref[...] + down_part(sources, down_ref, own_width)
    out_ref[...] = dot(spread[:, :slots], (total * share).astype(jnp.bfloat16)).astype(jnp.bfloat16)


def finish_kernel(resid_ref, arrived_ref, out_ref):
    subs, devs = lax.axis_size("sub"), lax.axis_size("dev")
    width = arrived_ref.shape[2]
    for s in range(subs):
        lanes = slice(s * width, (s + 1) * width)
        mixture = arrived_ref[s].astype(jnp.float32)
        for d in range(1, devs):
            mixture = mixture + arrived_ref[d * subs + s].astype(jnp.float32)
        out_ref[:, lanes] = (resid_ref[:, lanes].astype(jnp.float32) + mixture).astype(jnp.bfloat16)


def flip(x, axis, bits):
    return lax.ppermute(x, axis, [(i, i ^ bits) for i in range(lax.axis_size(axis))])


def per_device(
    tokens,
    queries,
    request_key_cache,
    request_value_cache,
    lengths,
    norm_gain,
    router_weight,
    routes,
    gate_weight,
    up_weight,
    down_weight,
):
    rows, width = tokens.shape
    devs, subs = lax.axis_size("dev"), lax.axis_size("sub")
    all_rows = rows * devs * subs
    slots = devs * (5 * rows * subs // 6)
    own_hidden = gate_weight.shape[1]
    out_width = down_weight.shape[1]
    bf16 = jnp.bfloat16
    opening = call(
        opening_kernel,
        jax.ShapeDtypeStruct((8, 128), jnp.float32),
        (),
        [],
        flops=OPENING_FLOPS,
        vmem=MIB,
    )
    operands = (
        opening,
        lengths,
        routes.T,
        queries,
        request_key_cache,
        request_value_cache,
        tokens,
        norm_gain,
        router_weight.T,
    )
    payload, resid = call(
        attention_kernel,
        (
            jax.ShapeDtypeStruct((rows, width + EXTRA), bf16),
            jax.ShapeDtypeStruct((rows, width), bf16),
        ),
        operands,
        [VMEM_SPEC, SMEM_SPEC, SMEM_SPEC] + [VMEM_SPEC] * 6,
        flops=30 * 10**9,
        bytes_accessed=100 * MIB,
        vmem=8 * MIB,
        scratch=[pltpu.VMEM((rows, width), jnp.float32)],
    )
    over_z = [payload] + [flip(payload, "dev", k) for k in (1, 2, 3)]
    over_x = [flip(p, "sub", 2) for p in over_z]
    over_core = [[flip(p, "sub", 1) for p in group] for group in (over_z, over_x)]
    pieces = []
    for k in range(devs):
        pieces += [over_z[k], over_core[0][k], over_x[k], over_core[1][k]]
    half = own_hidden // 2
    x, extra, hidden_a = call(
        lambda *refs: first_hidden_kernel(len(pieces), slots, *refs),
        (
            jax.ShapeDtypeStruct((slots, width), bf16),
            jax.ShapeDtypeStruct((all_rows, EXTRA), bf16),
            jax.ShapeDtypeStruct((slots, half), bf16),
        ),
        (*pieces, gate_weight, up_weight),
        [VMEM_SPEC] * (len(pieces) + 2),
        flops=2 * 10**9,
        vmem=6 * MIB,
        scratch=[pltpu.VMEM((all_rows, width + EXTRA), bf16)],
    )
    hidden_b = call(
        lambda *refs: next_hidden_kernel(half, *refs),
        jax.ShapeDtypeStruct((slots, own_hidden - half), bf16),
        (x, gate_weight, up_weight),
        [VMEM_SPEC] * 3,
        flops=2 * 10**9,
        vmem=4 * MIB,
    )
    far_a, near_a = flip(hidden_a, "sub", 2), flip(hidden_a, "sub", 1)
    far_b, near_b = flip(hidden_b, "sub", 2), flip(hidden_b, "sub", 1)
    across_a, across_b = flip(far_a, "sub", 1), flip(far_b, "sub", 1)
    total_shape = jax.ShapeDtypeStruct((slots, out_width), jnp.float32)
    flips = ((0, 0), (0, half), (1, 0), (1, half))
    total = call(
        lambda *refs: down_kernel(flips, own_hidden, False, *refs),
        total_shape,
        (hidden_a, hidden_b, near_a, near_b, down_weight),
        [VMEM_SPEC] * 5,
        flops=10**9,
        vmem=4 * MIB,
    )
    flips_a = ((2, 0), (3, 0))
    total = call(
        lambda *refs: down_kernel(flips_a, own_hidden, True, *refs),
        total_shape,
        (far_a, across_a, down_weight, total),
        [VMEM_SPEC] * 4,
        flops=10**9,
        vmem=4 * MIB,
    )
    flips_b = ((2, half), (3, half))
    weighted = call(
        lambda *refs: last_down_kernel(flips_b, own_hidden, rows, *refs),
        jax.ShapeDtypeStruct((all_rows, out_width), bf16),
        (far_b, across_b, down_weight, total, extra),
        [VMEM_SPEC] * 5,
        flops=10**9,
        vmem=4 * MIB,
    )
    arrived = lax.all_to_all(
        weighted.reshape(devs * subs, rows, out_width),
        ("dev", "sub"),
        split_axis=0,
        concat_axis=0,
        tiled=True,
    )
    return call(
        finish_kernel,
        jax.ShapeDtypeStruct((rows, width), bf16),
        (resid, arrived),
        [VMEM_SPEC] * 2,
        flops=10**6,
        vmem=4 * MIB,
    )


def solution(mesh):
    in_specs = (
        P(("rep", "dev", "sub"), None),
        P(("rep", "dev", "sub"), None),
        P(("rep", "dev", "sub"), None, None),
        P(("rep", "dev", "sub"), None, None),
        P(("rep", "dev", "sub")),
        P(),
        P(),
        P(("rep", "dev"), None),
        P(None, ("dev", "sub")),
        P(None, ("dev", "sub")),
        P("dev", "sub"),
    )
    out_specs = P(("rep", "dev", "sub"), None)
    one_expert_each = mesh.shape["dev"] == EXPERTS and mesh.shape["sub"] == 4
    return jax.shard_map(
        per_device if one_expert_each else general_plan,
        mesh=mesh,
        in_specs=in_specs,
        out_specs=out_specs,
        check_vma=False,
    )
```

```python
import functools
import math

import jax
import jax.numpy as jnp
from jax import lax
from jax.experimental import pallas as pl
from jax.experimental.pallas import tpu as pltpu
from jax.sharding import PartitionSpec as P

HEAD_SIZE = 128
QUERY_HEADS = 24
KEY_VALUE_HEADS = 4
EXPERTS = 4


def general_plan(
    tokens,
    queries,
    request_key_cache,
    request_value_cache,
    lengths,
    norm_gain,
    router_weight,
    routes,
    gate_weight,
    up_weight,
    down_weight,
):
    token_count = tokens.shape[0]
    feat_width = tokens.shape[1]
    cache_length = request_key_cache.shape[1]
    device_group = QUERY_HEADS // KEY_VALUE_HEADS
    query_tensor_four = queries.reshape(token_count, KEY_VALUE_HEADS, device_group, HEAD_SIZE)
    key_tensor_four = request_key_cache.reshape(
        token_count, cache_length, KEY_VALUE_HEADS, HEAD_SIZE
    )
    value_tensor_four = request_value_cache.reshape(
        token_count, cache_length, KEY_VALUE_HEADS, HEAD_SIZE
    )
    scores = jnp.einsum(
        "thgd,tchd->thgc", query_tensor_four, key_tensor_four, preferred_element_type=jnp.float32
    ) * (1.0 / math.sqrt(HEAD_SIZE))
    in_cache = (jnp.arange(cache_length)[None, :] < lengths[:, None])[:, None, None, :]
    scores = jnp.where(in_cache, scores, -jnp.inf)
    peak_score = jnp.max(scores, axis=-1, keepdims=True)
    exp_scores = jnp.exp(scores - peak_score)
    weights_bf = (exp_scores / jnp.sum(exp_scores, axis=-1, keepdims=True)).astype(jnp.bfloat16)
    attended = jnp.einsum(
        "thgc,tchd->thgd", weights_bf, value_tensor_four, preferred_element_type=jnp.float32
    ).reshape(token_count, feat_width)
    resid = (tokens.astype(jnp.float32) + attended).astype(jnp.bfloat16)
    resid_f = resid.astype(jnp.float32)
    stats = jnp.mean(resid_f * resid_f, axis=-1, keepdims=True)
    normed = (resid_f * lax.rsqrt(stats + 1e-05) * norm_gain.astype(jnp.float32)).astype(
        jnp.bfloat16
    )
    logits = jnp.dot(normed, router_weight, preferred_element_type=jnp.float32)
    sub_index = lax.axis_index("sub")
    sub_count = lax.axis_size("sub")
    dev_count = lax.axis_size("dev")
    expert_ids = jnp.arange(EXPERTS)
    own_routes = lax.dynamic_slice_in_dim(routes, sub_index * token_count, token_count, 0)
    first_logit = jnp.sum(jnp.where(own_routes[:, 0:1] == expert_ids[None, :], logits, 0.0), axis=1)
    second_logit = jnp.sum(
        jnp.where(own_routes[:, 1:2] == expert_ids[None, :], logits, 0.0), axis=1
    )
    first_share = jax.nn.sigmoid(first_logit - second_logit)
    second_share = jax.nn.sigmoid(second_logit - first_logit)
    block_rows = lax.all_gather(normed, "sub", axis=0, tiled=True)
    block_len = token_count * sub_count
    capacity = 5 * block_len // 6
    group_size = dev_count // EXPERTS
    flat_ids = routes.reshape(-1)
    route_hot = (flat_ids[:, None] == expert_ids[None, :]).astype(jnp.int32)
    earlier = jnp.cumsum(route_hot, axis=0) - route_hot
    slot_number = jnp.sum(earlier * route_hot, axis=1)
    slot_index = (flat_ids * capacity + slot_number).reshape(block_len, 2)
    slot_range = jnp.arange(EXPERTS * capacity)
    place_matrix = jnp.any(slot_index[None, :, :] == slot_range[:, None, None], axis=-1).astype(
        jnp.bfloat16
    )
    slot_total = dev_count * capacity
    packed = jnp.dot(place_matrix, block_rows, preferred_element_type=jnp.float32).astype(
        jnp.bfloat16
    )
    outgoing = jnp.repeat(packed.reshape(EXPERTS, capacity, feat_width), group_size, axis=0)
    arrived = lax.all_to_all(outgoing, "dev", split_axis=0, concat_axis=0, tiled=True).reshape(
        slot_total, feat_width
    )
    gate_part = jnp.dot(arrived, gate_weight, preferred_element_type=jnp.float32)
    up_part = jnp.dot(arrived, up_weight, preferred_element_type=jnp.float32)
    hidden = (jax.nn.silu(gate_part) * up_part).astype(jnp.bfloat16)
    out_width = down_weight.shape[1]
    partial_out = jnp.dot(
        lax.all_gather(hidden, "sub", axis=1, tiled=True),
        down_weight,
        preferred_element_type=jnp.float32,
    )
    returned = lax.all_to_all(
        partial_out.reshape(dev_count, capacity, out_width),
        "dev",
        split_axis=0,
        concat_axis=0,
        tiled=True,
    )
    expert_out = jnp.sum(
        returned.reshape(EXPERTS, group_size, capacity, out_width), axis=1
    ).reshape(EXPERTS * capacity, out_width)
    pick_matrix = (slot_index.reshape(-1)[:, None] == slot_range[None, :]).astype(jnp.float32)
    per_route = jnp.dot(pick_matrix, expert_out, precision=lax.Precision.HIGHEST).reshape(
        block_len, 2, out_width
    )
    own_outputs = lax.all_to_all(per_route, "sub", split_axis=0, concat_axis=2, tiled=True)
    mixture = (
        first_share[:, None] * own_outputs[:, 0, :] + second_share[:, None] * own_outputs[:, 1, :]
    )
    return (resid_f + mixture).astype(jnp.bfloat16)


VMEM_SPEC = pl.BlockSpec(memory_space=pltpu.VMEM)
SMEM_SPEC = pl.BlockSpec(memory_space=pltpu.SMEM)
MIB = 1024 * 1024
CHUNKS = (4, 4, 4, 4)
Z_ORDER = (3, 2, 1)
EARLY, LATE = (1, 3), (0, 2)
PACK_FLOPS = 10**8
OPENING_FLOPS = 4 * 10**9
ATTENTION_FLOPS = 30 * 10**9
GATE_FLOPS = 10**9
DOWN_FLOPS = 10**9
EXTRA = 128


def call(body, out_shapes, operands, specs, flops, vmem, scratch=(), bytes_accessed=0):
    return pl.pallas_call(
        body,
        out_shape=out_shapes,
        in_specs=specs,
        out_specs=jax.tree.map(lambda _: VMEM_SPEC, out_shapes),
        scratch_shapes=list(scratch),
        compiler_params=pltpu.CompilerParams(vmem_limit_bytes=vmem),
        cost_estimate=pl.CostEstimate(
            flops=flops, bytes_accessed=bytes_accessed, transcendentals=0
        ),
    )(*operands)


def dot(a, b):
    return jnp.dot(a, b, preferred_element_type=jnp.float32)


def dot_nt(a, b):
    return lax.dot_general(a, b, (((1,), (1,)), ((), ())), preferred_element_type=jnp.float32)


def opening_kernel(out_ref):
    out_ref[...] = jnp.zeros_like(out_ref)


def attention_kernel(
    _,
    lengths_ref,
    routes_ref,
    queries_ref,
    keys_ref,
    values_ref,
    tokens_ref,
    gain_ref,
    payload_ref,
    resid_ref,
    att_ref,
):
    rows, width = tokens_ref.shape
    cache = keys_ref.shape[1]
    group = QUERY_HEADS // KEY_VALUE_HEADS
    row = lax.broadcasted_iota(jnp.int32, (rows, 1), 0)
    live = jnp.zeros((rows, 1), jnp.int32)
    first = jnp.zeros((rows, 1), jnp.int32)
    second = jnp.zeros((rows, 1), jnp.int32)
    base = lax.axis_index("sub") * rows
    for t in range(rows):
        live = jnp.where(row == t, lengths_ref[t], live)
        first = jnp.where(row == t, routes_ref[0, base + t], first)
        second = jnp.where(row == t, routes_ref[1, base + t], second)
    column = lax.broadcasted_iota(jnp.int32, (rows, rows * cache), 1)
    start = row * cache
    in_cache = (column >= start) & (column < start + live)
    in_cache = jnp.concatenate([in_cache.astype(jnp.int32)] * group, axis=0) > 0
    scale = 1.0 / math.sqrt(HEAD_SIZE)
    for kv in range(KEY_VALUE_HEADS):
        heads = [queries_ref[:, h * HEAD_SIZE : (h + 1) * HEAD_SIZE].astype(jnp.float32)
                 for h in range(kv * group, (kv + 1) * group)]
        query = jnp.concatenate(heads, axis=0).astype(jnp.bfloat16)
        lanes = slice(kv * HEAD_SIZE, (kv + 1) * HEAD_SIZE)
        key = keys_ref[:, :, lanes].reshape(rows * cache, HEAD_SIZE)
        value = values_ref[:, :, lanes].reshape(rows * cache, HEAD_SIZE)
        scores = jnp.where(in_cache, dot_nt(query, key) * scale, -jnp.inf)
        exp_scores = jnp.exp(scores - jnp.max(scores, axis=1, keepdims=True))
        total = jnp.sum(exp_scores, axis=1, keepdims=True)
        probs = (exp_scores * (1.0 / total)).astype(jnp.bfloat16)
        attended = dot(probs, value)
        for g in range(group):
            h = kv * group + g
            att_ref[:, h * HEAD_SIZE : (h + 1) * HEAD_SIZE] = attended[g * rows : (g + 1) * rows]
    resid = (tokens_ref[...].astype(jnp.float32) + att_ref[...]).astype(jnp.bfloat16)
    resid_ref[...] = resid
    resid_f = resid.astype(jnp.float32)
    stats = jnp.sum(resid_f * resid_f, axis=1, keepdims=True) * (1.0 / width)
    gain = gain_ref[...].astype(jnp.float32).reshape(1, width)
    normed = (resid_f * lax.rsqrt(stats + 1e-05) * gain).astype(jnp.bfloat16)
    payload_ref[:, :width] = normed
    lane = lax.broadcasted_iota(jnp.int32, (rows, EXTRA), 1)
    routed = ((first == lane) | (second == lane)).astype(jnp.float32)
    payload_ref[:, width:] = routed.astype(jnp.bfloat16)


def own_offset(rows):
    return lax.axis_index("sub") * rows


def slot_matrix(extra, offset, block_rows, blocks, cap):
    count = extra.shape[0]
    here = lax.broadcasted_iota(jnp.int32, (count, count), 0)
    there = lax.broadcasted_iota(jnp.int32, (count, count), 1)
    before = (there // block_rows == here // block_rows) & ((there ^ offset) < (here ^ offset))
    earlier = dot(before.astype(jnp.bfloat16), extra)
    lane = lax.broadcasted_iota(jnp.int32, (count, EXTRA), 1)
    mine = lane == lax.axis_index("dev")
    rank = jnp.sum(jnp.where(mine, earlier, 0.0), axis=1, keepdims=True)
    routed = jnp.sum(jnp.where(mine, extra.astype(jnp.float32), 0.0), axis=1, keepdims=True)
    block = lax.broadcasted_iota(jnp.int32, (count, 1), 0) // block_rows
    base = jnp.zeros((count, 1), jnp.int32)
    for i, k in enumerate(blocks):
        base = jnp.where(block == i, k * cap, base)
    slot = jnp.where(routed > 0.5, rank.astype(jnp.int32) + base, -1)
    return (slot == lax.broadcasted_iota(jnp.int32, (count, EXTRA), 1)).astype(jnp.float32)


def hidden_columns(x, gate_ref, up_ref, out_ref, begin):
    step = min(256, out_ref.shape[1])
    end = out_ref.shape[1]
    for j in range(0, end, step):
        columns = slice(begin + j, begin + min(j + step, end))
        gate = dot(x, gate_ref[:, columns])
        up = dot(x, up_ref[:, columns])
        out_ref[:, j : min(j + step, end)] = (gate / (1.0 + jnp.exp(-gate)) * up).astype(jnp.bfloat16)


def join(piece_refs, rows_ref):
    at = 0
    for first, second in zip(piece_refs[0::2], piece_refs[1::2], strict=True):
        both = [first[...].astype(jnp.float32), second[...].astype(jnp.float32)]
        size = first.shape[0] + second.shape[0]
        rows_ref[at : at + size, :] = jnp.concatenate(both, axis=0).astype(jnp.bfloat16)
        at += size


def placed(rows_ref, width, piece_rows, blocks, cap, slots):
    block_rows = rows_ref.shape[0] // len(blocks)
    place = slot_matrix(rows_ref[:, width:], own_offset(piece_rows), block_rows, blocks, cap)
    return dot(place.T[:slots].astype(jnp.bfloat16), rows_ref[:, :width])


def pack_kernel(pieces, blocks, cap, *refs):
    x_ref, extra_ref, rows_ref = refs[pieces:]
    slots, width = x_ref.shape
    join(refs[:pieces], rows_ref)
    extra_ref[...] = rows_ref[:, width:]
    x_ref[...] = placed(rows_ref, width, refs[0].shape[0], blocks, cap, slots).astype(jnp.bfloat16)


def first_hidden_kernel(pieces, blocks, cap, *refs):
    packed_ref, gate_ref, up_ref, x_ref, extra_ref, hidden_ref, rows_ref = refs[pieces:]
    slots, width = x_ref.shape
    join(refs[:pieces], rows_ref)
    extra_ref[...] = rows_ref[:, width:]
    late = placed(rows_ref, width, refs[0].shape[0], blocks, cap, slots)
    x_ref[...] = (packed_ref[...].astype(jnp.float32) + late).astype(jnp.bfloat16)
    hidden_columns(x_ref[...], gate_ref, up_ref, hidden_ref, 0)


def next_hidden_kernel(begin, x_ref, gate_ref, up_ref, hidden_ref):
    hidden_columns(x_ref[...], gate_ref, up_ref, hidden_ref, begin)


def down_part(sources, down_ref, own_width):
    sub = lax.axis_index("sub")
    total = None
    for hidden_ref, flip, begin in sources:
        height = hidden_ref.shape[1]
        at = pl.multiple_of((sub ^ flip) * own_width + begin, 128)
        part = dot(hidden_ref[...], down_ref[pl.ds(at, height), :])
        total = part if total is None else total + part
    return total


def down_kernel(flips, own_width, has_total, *refs):
    count = len(flips)
    hidden_refs = refs[:count]
    rest = refs[count:]
    sources = [(r, f, b) for r, (f, b) in zip(hidden_refs, flips, strict=True)]
    total = down_part(sources, rest[0], own_width)
    if has_total:
        total = total + rest[1][...]
    rest[-1][...] = total


def return_kernel(rows, order, cap, *refs):
    *extra_refs, x_ref, router_ref, spread_ref, share_ref = refs
    slots = share_ref.shape[0]
    extra = jnp.concatenate([ref[...] for ref in extra_refs], axis=0)
    here = slot_matrix(extra, own_offset(rows), extra.shape[0] // len(order), order, cap)
    spread_ref[...] = here.astype(jnp.bfloat16)
    routed = dot(here.T[:slots].astype(jnp.bfloat16), extra)[:, :EXPERTS] > 0.5
    logits = dot_nt(x_ref[...], router_ref[...])
    mine = lax.broadcasted_iota(jnp.int32, logits.shape, 1) == lax.axis_index("dev")
    own_logit = jnp.sum(jnp.where(mine, logits, 0.0), axis=1, keepdims=True)
    other_logit = jnp.sum(jnp.where(routed & ~mine, logits, 0.0), axis=1, keepdims=True)
    share = 1.0 / (1.0 + jnp.exp(other_logit - own_logit))
    share_ref[...] = jnp.broadcast_to(share, share_ref.shape)


def last_down_kernel(flips, own_width, *refs):
    count = len(flips)
    hidden_refs = refs[:count]
    down_ref, total_ref, spread_ref, share_ref, *out_refs = refs[count:]
    sources = [(r, f, b) for r, (f, b) in zip(hidden_refs, flips, strict=True)]
    slots = total_ref.shape[0]
    total = total_ref[...] + down_part(sources, down_ref, own_width)
    weighted = (total * share_ref[:, :1]).astype(jnp.bfloat16)
    result = dot(spread_ref[:, :slots], weighted).astype(jnp.bfloat16)
    height = out_refs[0].shape[0]
    for k, out_ref in enumerate(out_refs):
        out_ref[...] = result[k * height : (k + 1) * height]


def collect_kernel(rows, *refs):
    parts, (own_ref, *out_refs) = refs[:-4], refs[-4:]
    total = parts[0][...].astype(jnp.float32)
    for part in parts[1:]:
        total = total + part[...].astype(jnp.float32)
    own_ref[...] = total[:rows]
    for i, out_ref in enumerate(out_refs):
        out_ref[...] = total[(i + 1) * rows : (i + 2) * rows].astype(jnp.bfloat16)


def finish_kernel(resid_ref, *refs):
    *mixture_refs, out_ref = refs
    width = mixture_refs[0].shape[1]
    sub = lax.axis_index("sub")
    for bits, mixture_ref in enumerate(mixture_refs):
        lanes = pl.ds(pl.multiple_of((sub ^ bits) * width, 128), width)
        mixture = mixture_ref[...].astype(jnp.float32)
        out_ref[:, lanes] = (resid_ref[:, lanes].astype(jnp.float32) + mixture).astype(jnp.bfloat16)


def flip(x, axis, bits):
    return lax.ppermute(x, axis, [(i, i ^ bits) for i in range(lax.axis_size(axis))])


def per_device(
    tokens,
    queries,
    request_key_cache,
    request_value_cache,
    lengths,
    norm_gain,
    router_weight,
    routes,
    gate_weight,
    up_weight,
    down_weight,
):
    rows, width = tokens.shape
    devs, subs = lax.axis_size("dev"), lax.axis_size("sub")
    all_rows = rows * devs * subs
    cap = 5 * rows * subs // 6
    slots = devs * cap
    own_hidden = gate_weight.shape[1]
    out_width = down_weight.shape[1]
    bf16 = jnp.bfloat16
    opening = call(
        opening_kernel,
        jax.ShapeDtypeStruct((8, 128), jnp.float32),
        (),
        [],
        flops=OPENING_FLOPS,
        vmem=MIB,
    )
    operands = (
        opening,
        lengths,
        routes.T,
        queries,
        request_key_cache,
        request_value_cache,
        tokens,
        norm_gain,
    )
    payload, resid = call(
        attention_kernel,
        (
            jax.ShapeDtypeStruct((rows, width + EXTRA), bf16),
            jax.ShapeDtypeStruct((rows, width), bf16),
        ),
        operands,
        [VMEM_SPEC, SMEM_SPEC, SMEM_SPEC] + [VMEM_SPEC] * 5,
        flops=ATTENTION_FLOPS,
        bytes_accessed=100 * MIB,
        vmem=8 * MIB,
        scratch=[pltpu.VMEM((rows, width), jnp.float32)],
    )
    over_z = [payload] + [flip(payload, "dev", k) for k in range(1, devs)]
    over_x = [flip(p, "sub", 2) for p in over_z]
    pieces = [[z, flip(z, "sub", 1), x, flip(x, "sub", 1)] for z, x in zip(over_z, over_x, strict=True)]
    unit = own_hidden // 16
    widths = [unit * n for n in CHUNKS]
    begins = [sum(widths[:i]) for i in range(len(widths))]
    chunks = len(widths)
    early = [p for k in EARLY for p in pieces[k]]
    block_rows = all_rows // devs
    early_rows = block_rows * len(EARLY)
    packed, extra_early = call(
        functools.partial(pack_kernel, len(early), EARLY, cap),
        (
            jax.ShapeDtypeStruct((slots, width), bf16),
            jax.ShapeDtypeStruct((early_rows, EXTRA), bf16),
        ),
        early,
        [VMEM_SPEC] * len(early),
        flops=PACK_FLOPS,
        vmem=6 * MIB,
        scratch=[pltpu.VMEM((early_rows, width + EXTRA), bf16)],
    )
    late = [p for k in LATE for p in pieces[k]]
    late_rows = block_rows * len(LATE)
    x, extra_late, hidden = call(
        functools.partial(first_hidden_kernel, len(late), LATE, cap),
        (
            jax.ShapeDtypeStruct((slots, width), bf16),
            jax.ShapeDtypeStruct((late_rows, EXTRA), bf16),
            jax.ShapeDtypeStruct((slots, widths[0]), bf16),
        ),
        (*late, packed, gate_weight, up_weight),
        [VMEM_SPEC] * (len(late) + 3),
        flops=GATE_FLOPS,
        vmem=6 * MIB,
        scratch=[pltpu.VMEM((late_rows, width + EXTRA), bf16)],
    )
    own = [hidden]
    for i in range(1, chunks):
        own.append(
            call(
                functools.partial(next_hidden_kernel, begins[i]),
                jax.ShapeDtypeStruct((slots, widths[i]), bf16),
                (x, gate_weight, up_weight),
                [VMEM_SPEC] * 3,
                flops=GATE_FLOPS,
                vmem=4 * MIB,
            )
        )
    far = [flip(h, "sub", 2) for h in own]
    near = [flip(h, "sub", 1) for h in own]
    across = [flip(h, "sub", 1) for h in far]
    spread, share = call(
        functools.partial(return_kernel, rows, (*EARLY, *LATE), cap),
        (
            jax.ShapeDtypeStruct((all_rows, EXTRA), bf16),
            jax.ShapeDtypeStruct((slots, EXTRA), jnp.float32),
        ),
        (extra_early, extra_late, x, router_weight.T),
        [VMEM_SPEC] * 4,
        flops=DOWN_FLOPS,
        vmem=4 * MIB,
    )
    total_shape = jax.ShapeDtypeStruct((slots, out_width), jnp.float32)
    total = None
    for i in range(chunks):
        taken = [near[i], far[i], across[i]]
        flips = [(1, begins[i]), (2, begins[i]), (3, begins[i])]
        if i < chunks - 1:
            taken.append(own[i])
            flips.append((0, begins[i]))
        if i == chunks - 2:
            taken.append(own[i + 1])
            flips.append((0, begins[i + 1]))
        before = () if total is None else (total,)
        if i < chunks - 1:
            total = call(
                functools.partial(down_kernel, flips, own_hidden, i > 0),
                total_shape,
                (*taken, down_weight, *before),
                [VMEM_SPEC] * (len(taken) + 1 + len(before)),
                flops=DOWN_FLOPS,
                vmem=4 * MIB,
            )
        else:
            weighted = call(
                functools.partial(last_down_kernel, flips, own_hidden),
                (jax.ShapeDtypeStruct((all_rows // devs, out_width), bf16),) * devs,
                (*taken, down_weight, total, spread, share),
                [VMEM_SPEC] * (len(taken) + 4),
                flops=DOWN_FLOPS,
                vmem=4 * MIB,
            )
    weighted = dict(zip((*EARLY, *LATE), weighted, strict=True))
    arrived = [weighted[0]] + [flip(weighted[k], "dev", k) for k in Z_ORDER]
    mixed, to_near, to_far, to_across = call(
        functools.partial(collect_kernel, rows),
        (jax.ShapeDtypeStruct((rows, out_width), jnp.float32),)
        + (jax.ShapeDtypeStruct((rows, out_width), bf16),) * 3,
        arrived,
        [VMEM_SPEC] * devs,
        flops=10**6,
        vmem=4 * MIB,
    )
    from_across = flip(flip(to_across, "sub", 1), "sub", 2)
    from_near = flip(to_near, "sub", 1)
    from_far = flip(to_far, "sub", 2)
    return call(
        finish_kernel,
        jax.ShapeDtypeStruct((rows, width), bf16),
        (resid, mixed, from_near, from_far, from_across),
        [VMEM_SPEC] * 5,
        flops=10**6,
        vmem=4 * MIB,
    )


def solution(mesh):
    in_specs = (
        P(("rep", "dev", "sub"), None),
        P(("rep", "dev", "sub"), None),
        P(("rep", "dev", "sub"), None, None),
        P(("rep", "dev", "sub"), None, None),
        P(("rep", "dev", "sub")),
        P(),
        P(),
        P(("rep", "dev"), None),
        P(None, ("dev", "sub")),
        P(None, ("dev", "sub")),
        P("dev", "sub"),
    )
    out_specs = P(("rep", "dev", "sub"), None)
    one_expert_each = mesh.shape["dev"] == EXPERTS and mesh.shape["sub"] == 4
    return jax.shard_map(
        per_device if one_expert_each else general_plan,
        mesh=mesh,
        in_specs=in_specs,
        out_specs=out_specs,
        check_vma=False,
    )
```

```python
import functools
import math

import jax
import jax.numpy as jnp
from jax import lax
from jax.experimental import pallas as pl
from jax.experimental.pallas import tpu as pltpu
from jax.sharding import PartitionSpec as P

HEAD_SIZE = 128
QUERY_HEADS = 24
KEY_VALUE_HEADS = 4
EXPERTS = 4


def general_plan(
    tokens,
    queries,
    request_key_cache,
    request_value_cache,
    lengths,
    norm_gain,
    router_weight,
    routes,
    gate_weight,
    up_weight,
    down_weight,
):
    token_count = tokens.shape[0]
    feat_width = tokens.shape[1]
    cache_length = request_key_cache.shape[1]
    device_group = QUERY_HEADS // KEY_VALUE_HEADS
    query_tensor_four = queries.reshape(token_count, KEY_VALUE_HEADS, device_group, HEAD_SIZE)
    key_tensor_four = request_key_cache.reshape(
        token_count, cache_length, KEY_VALUE_HEADS, HEAD_SIZE
    )
    value_tensor_four = request_value_cache.reshape(
        token_count, cache_length, KEY_VALUE_HEADS, HEAD_SIZE
    )
    scores = jnp.einsum(
        "thgd,tchd->thgc", query_tensor_four, key_tensor_four, preferred_element_type=jnp.float32
    ) * (1.0 / math.sqrt(HEAD_SIZE))
    in_cache = (jnp.arange(cache_length)[None, :] < lengths[:, None])[:, None, None, :]
    scores = jnp.where(in_cache, scores, -jnp.inf)
    peak_score = jnp.max(scores, axis=-1, keepdims=True)
    exp_scores = jnp.exp(scores - peak_score)
    weights_bf = (exp_scores / jnp.sum(exp_scores, axis=-1, keepdims=True)).astype(jnp.bfloat16)
    attended = jnp.einsum(
        "thgc,tchd->thgd", weights_bf, value_tensor_four, preferred_element_type=jnp.float32
    ).reshape(token_count, feat_width)
    resid = (tokens.astype(jnp.float32) + attended).astype(jnp.bfloat16)
    resid_f = resid.astype(jnp.float32)
    stats = jnp.mean(resid_f * resid_f, axis=-1, keepdims=True)
    normed = (resid_f * lax.rsqrt(stats + 1e-05) * norm_gain.astype(jnp.float32)).astype(
        jnp.bfloat16
    )
    logits = jnp.dot(normed, router_weight, preferred_element_type=jnp.float32)
    sub_index = lax.axis_index("sub")
    sub_count = lax.axis_size("sub")
    dev_count = lax.axis_size("dev")
    expert_ids = jnp.arange(EXPERTS)
    own_routes = lax.dynamic_slice_in_dim(routes, sub_index * token_count, token_count, 0)
    first_logit = jnp.sum(jnp.where(own_routes[:, 0:1] == expert_ids[None, :], logits, 0.0), axis=1)
    second_logit = jnp.sum(
        jnp.where(own_routes[:, 1:2] == expert_ids[None, :], logits, 0.0), axis=1
    )
    first_share = jax.nn.sigmoid(first_logit - second_logit)
    second_share = jax.nn.sigmoid(second_logit - first_logit)
    block_rows = lax.all_gather(normed, "sub", axis=0, tiled=True)
    block_len = token_count * sub_count
    capacity = 5 * block_len // 6
    group_size = dev_count // EXPERTS
    flat_ids = routes.reshape(-1)
    route_hot = (flat_ids[:, None] == expert_ids[None, :]).astype(jnp.int32)
    earlier = jnp.cumsum(route_hot, axis=0) - route_hot
    slot_number = jnp.sum(earlier * route_hot, axis=1)
    slot_index = (flat_ids * capacity + slot_number).reshape(block_len, 2)
    slot_range = jnp.arange(EXPERTS * capacity)
    place_matrix = jnp.any(slot_index[None, :, :] == slot_range[:, None, None], axis=-1).astype(
        jnp.bfloat16
    )
    slot_total = dev_count * capacity
    packed = jnp.dot(place_matrix, block_rows, preferred_element_type=jnp.float32).astype(
        jnp.bfloat16
    )
    outgoing = jnp.repeat(packed.reshape(EXPERTS, capacity, feat_width), group_size, axis=0)
    arrived = lax.all_to_all(outgoing, "dev", split_axis=0, concat_axis=0, tiled=True).reshape(
        slot_total, feat_width
    )
    gate_part = jnp.dot(arrived, gate_weight, preferred_element_type=jnp.float32)
    up_part = jnp.dot(arrived, up_weight, preferred_element_type=jnp.float32)
    hidden = (jax.nn.silu(gate_part) * up_part).astype(jnp.bfloat16)
    out_width = down_weight.shape[1]
    partial_out = jnp.dot(
        lax.all_gather(hidden, "sub", axis=1, tiled=True),
        down_weight,
        preferred_element_type=jnp.float32,
    )
    returned = lax.all_to_all(
        partial_out.reshape(dev_count, capacity, out_width),
        "dev",
        split_axis=0,
        concat_axis=0,
        tiled=True,
    )
    expert_out = jnp.sum(
        returned.reshape(EXPERTS, group_size, capacity, out_width), axis=1
    ).reshape(EXPERTS * capacity, out_width)
    pick_matrix = (slot_index.reshape(-1)[:, None] == slot_range[None, :]).astype(jnp.float32)
    per_route = jnp.dot(pick_matrix, expert_out, precision=lax.Precision.HIGHEST).reshape(
        block_len, 2, out_width
    )
    own_outputs = lax.all_to_all(per_route, "sub", split_axis=0, concat_axis=2, tiled=True)
    mixture = (
        first_share[:, None] * own_outputs[:, 0, :] + second_share[:, None] * own_outputs[:, 1, :]
    )
    return (resid_f + mixture).astype(jnp.bfloat16)


VMEM_SPEC = pl.BlockSpec(memory_space=pltpu.VMEM)
SMEM_SPEC = pl.BlockSpec(memory_space=pltpu.SMEM)
MIB = 1024 * 1024
CHUNKS = (4, 4, 4, 4)
Z_ORDER = (3, 2, 1)
EARLY, LATE = (1, 3), (0, 2)
PAIRED = 0
LAST_FLOPS = 10**9
PACK_FLOPS = 10**8
OPENING_FLOPS = 6 * 10**9
ATTENTION_FLOPS = 30 * 10**9
GATE_FLOPS = 10**9
DOWN_FLOPS = 10**9
EXTRA = 128


def call(body, out_shapes, operands, specs, flops, vmem, scratch=(), bytes_accessed=0):
    return pl.pallas_call(
        body,
        out_shape=out_shapes,
        in_specs=specs,
        out_specs=jax.tree.map(lambda _: VMEM_SPEC, out_shapes),
        scratch_shapes=list(scratch),
        compiler_params=pltpu.CompilerParams(vmem_limit_bytes=vmem),
        cost_estimate=pl.CostEstimate(
            flops=flops, bytes_accessed=bytes_accessed, transcendentals=0
        ),
    )(*operands)


def dot(a, b):
    return jnp.dot(a, b, preferred_element_type=jnp.float32)


def dot_nt(a, b):
    return lax.dot_general(a, b, (((1,), (1,)), ((), ())), preferred_element_type=jnp.float32)


def opening_kernel(out_ref):
    out_ref[...] = jnp.zeros_like(out_ref)


def attention_kernel(
    _,
    lengths_ref,
    routes_ref,
    queries_ref,
    keys_ref,
    values_ref,
    tokens_ref,
    gain_ref,
    payload_ref,
    resid_ref,
    att_ref,
):
    rows, width = tokens_ref.shape
    cache = keys_ref.shape[1]
    group = QUERY_HEADS // KEY_VALUE_HEADS
    row = lax.broadcasted_iota(jnp.int32, (rows, 1), 0)
    live = jnp.zeros((rows, 1), jnp.int32)
    first = jnp.zeros((rows, 1), jnp.int32)
    second = jnp.zeros((rows, 1), jnp.int32)
    base = lax.axis_index("sub") * rows
    for t in range(rows):
        live = jnp.where(row == t, lengths_ref[t], live)
        first = jnp.where(row == t, routes_ref[0, base + t], first)
        second = jnp.where(row == t, routes_ref[1, base + t], second)
    column = lax.broadcasted_iota(jnp.int32, (rows, rows * cache), 1)
    start = row * cache
    in_cache = (column >= start) & (column < start + live)
    bias = jnp.where(in_cache, 0.0, -jnp.inf)[None]
    scale = 1.0 / math.sqrt(HEAD_SIZE)
    pair = 4
    for kv in range(0, KEY_VALUE_HEADS, pair):
        lanes = slice(kv * HEAD_SIZE, (kv + pair) * HEAD_SIZE)
        key = keys_ref[:, :, lanes].reshape(rows * cache, pair * HEAD_SIZE)
        value = values_ref[:, :, lanes].reshape(rows * cache, pair * HEAD_SIZE)
        queries = []
        blank = jnp.zeros((group * rows, HEAD_SIZE), jnp.float32)
        for one in range(pair):
            heads = [
                queries_ref[:, h * HEAD_SIZE : (h + 1) * HEAD_SIZE].astype(jnp.float32)
                for h in range((kv + one) * group, (kv + one + 1) * group)
            ]
            blocks = [blank] * pair
            blocks[one] = jnp.concatenate(heads, axis=0)
            queries.append(jnp.concatenate(blocks, axis=1))
        query = jnp.concatenate(queries, axis=0).astype(jnp.bfloat16)
        scores = dot_nt(query, key).reshape(pair * group, rows, rows * cache) * scale + bias
        exp_scores = jnp.exp(scores - jnp.max(scores, axis=2, keepdims=True))
        total = jnp.sum(exp_scores, axis=2, keepdims=True)
        probs = (exp_scores * (1.0 / total)).reshape(pair * group * rows, rows * cache)
        attended = dot(probs.astype(jnp.bfloat16), value)
        for n in range(pair * group):
            h = kv * group + n
            one = n // group
            att_ref[:, h * HEAD_SIZE : (h + 1) * HEAD_SIZE] = attended[
                n * rows : (n + 1) * rows, one * HEAD_SIZE : (one + 1) * HEAD_SIZE
            ]
    resid = (tokens_ref[...].astype(jnp.float32) + att_ref[...]).astype(jnp.bfloat16)
    resid_ref[...] = resid
    resid_f = resid.astype(jnp.float32)
    stats = jnp.sum(resid_f * resid_f, axis=1, keepdims=True) * (1.0 / width)
    gain = gain_ref[...].astype(jnp.float32).reshape(1, width)
    normed = (resid_f * lax.rsqrt(stats + 1e-05) * gain).astype(jnp.bfloat16)
    payload_ref[:, :width] = normed
    lane = lax.broadcasted_iota(jnp.int32, (rows, EXTRA), 1)
    routed = ((first == lane) | (second == lane)).astype(jnp.float32)
    payload_ref[:, width:] = routed.astype(jnp.bfloat16)


def own_offset(rows):
    return lax.axis_index("sub") * rows


def slot_matrix(extra, offset, block_rows, blocks, cap):
    count = extra.shape[0]
    here = lax.broadcasted_iota(jnp.int32, (count, count), 0)
    there = lax.broadcasted_iota(jnp.int32, (count, count), 1)
    before = (there // block_rows == here // block_rows) & ((there ^ offset) < (here ^ offset))
    earlier = dot(before.astype(jnp.bfloat16), extra)
    lane = lax.broadcasted_iota(jnp.int32, (count, EXTRA), 1)
    mine = lane == lax.axis_index("dev")
    rank = jnp.sum(jnp.where(mine, earlier, 0.0), axis=1, keepdims=True)
    routed = jnp.sum(jnp.where(mine, extra.astype(jnp.float32), 0.0), axis=1, keepdims=True)
    block = lax.broadcasted_iota(jnp.int32, (count, 1), 0) // block_rows
    base = jnp.zeros((count, 1), jnp.int32)
    for i, k in enumerate(blocks):
        base = jnp.where(block == i, k * cap, base)
    slot = jnp.where(routed > 0.5, rank.astype(jnp.int32) + base, -1)
    return (slot == lax.broadcasted_iota(jnp.int32, (count, EXTRA), 1)).astype(jnp.float32)


def hidden_columns(x, gate_ref, up_ref, out_ref, begin):
    step = min(256, out_ref.shape[1])
    end = out_ref.shape[1]
    for j in range(0, end, step):
        columns = slice(begin + j, begin + min(j + step, end))
        gate = dot(x, gate_ref[:, columns])
        up = dot(x, up_ref[:, columns])
        out_ref[:, j : min(j + step, end)] = (gate / (1.0 + jnp.exp(-gate)) * up).astype(jnp.bfloat16)


def join(piece_refs, rows_ref):
    at = 0
    for first, second in zip(piece_refs[0::2], piece_refs[1::2], strict=True):
        both = [first[...].astype(jnp.float32), second[...].astype(jnp.float32)]
        size = first.shape[0] + second.shape[0]
        rows_ref[at : at + size, :] = jnp.concatenate(both, axis=0).astype(jnp.bfloat16)
        at += size


def placed(rows_ref, width, piece_rows, blocks, cap, slots):
    block_rows = rows_ref.shape[0] // len(blocks)
    place = slot_matrix(rows_ref[:, width:], own_offset(piece_rows), block_rows, blocks, cap)
    return dot(place.T[:slots].astype(jnp.bfloat16), rows_ref[:, :width])


def pack_kernel(pieces, blocks, cap, *refs):
    x_ref, extra_ref, rows_ref = refs[pieces:]
    slots, width = x_ref.shape
    join(refs[:pieces], rows_ref)
    extra_ref[...] = rows_ref[:, width:]
    x_ref[...] = placed(rows_ref, width, refs[0].shape[0], blocks, cap, slots).astype(jnp.bfloat16)


def first_hidden_kernel(pieces, blocks, cap, *refs):
    packed_ref, gate_ref, up_ref, x_ref, extra_ref, hidden_ref, rows_ref = refs[pieces:]
    slots, width = x_ref.shape
    join(refs[:pieces], rows_ref)
    extra_ref[...] = rows_ref[:, width:]
    late = placed(rows_ref, width, refs[0].shape[0], blocks, cap, slots)
    x_ref[...] = (packed_ref[...].astype(jnp.float32) + late).astype(jnp.bfloat16)
    hidden_columns(x_ref[...], gate_ref, up_ref, hidden_ref, 0)


def next_hidden_kernel(begin, x_ref, gate_ref, up_ref, hidden_ref):
    hidden_columns(x_ref[...], gate_ref, up_ref, hidden_ref, begin)


def pair_kernel(first_ref, second_ref, out_ref):
    width = first_ref.shape[1]
    out_ref[:, :width] = first_ref[...]
    out_ref[:, width:] = second_ref[...]


def down_part(refs, sources, down_ref, own_width):
    sub = lax.axis_index("sub")
    total = None
    for which, start, width, bits, begin in sources:
        at = pl.multiple_of((sub ^ bits) * own_width + begin, 128)
        part = dot(refs[which][:, start : start + width], down_ref[pl.ds(at, width), :])
        total = part if total is None else total + part
    return total


def down_kernel(sources, own_width, has_total, *refs):
    rest = refs[-3:] if has_total else refs[-2:]
    total = down_part(refs, sources, rest[0], own_width)
    if has_total:
        total = total + rest[1][...]
    rest[-1][...] = total


def return_kernel(rows, order, cap, *refs):
    *extra_refs, x_ref, router_ref, spread_ref, share_ref = refs
    slots = share_ref.shape[0]
    extra = jnp.concatenate([ref[...] for ref in extra_refs], axis=0)
    here = slot_matrix(extra, own_offset(rows), extra.shape[0] // len(order), order, cap)
    spread_ref[...] = here.astype(jnp.bfloat16)
    routed = dot(here.T[:slots].astype(jnp.bfloat16), extra)[:, :EXPERTS] > 0.5
    logits = dot_nt(x_ref[...], router_ref[...])
    mine = lax.broadcasted_iota(jnp.int32, logits.shape, 1) == lax.axis_index("dev")
    own_logit = jnp.sum(jnp.where(mine, logits, 0.0), axis=1, keepdims=True)
    other_logit = jnp.sum(jnp.where(routed & ~mine, logits, 0.0), axis=1, keepdims=True)
    share = 1.0 / (1.0 + jnp.exp(other_logit - own_logit))
    share_ref[...] = jnp.broadcast_to(share, share_ref.shape)


def last_down_kernel(sources, operands, own_width, *refs):
    down_ref, total_ref, spread_ref, share_ref, *out_refs = refs[operands:]
    slots = total_ref.shape[0]
    total = total_ref[...] + down_part(refs, sources, down_ref, own_width)
    weighted = (total * share_ref[:, :1]).astype(jnp.bfloat16)
    result = dot(spread_ref[:, :slots], weighted).astype(jnp.bfloat16)
    height = out_refs[0].shape[0]
    for k, out_ref in enumerate(out_refs):
        out_ref[...] = result[k * height : (k + 1) * height]


def collect_kernel(rows, *refs):
    parts, (own_ref, *out_refs) = refs[:-4], refs[-4:]
    total = parts[0][...].astype(jnp.float32)
    for part in parts[1:]:
        total = total + part[...].astype(jnp.float32)
    own_ref[...] = total[:rows]
    for i, out_ref in enumerate(out_refs):
        out_ref[...] = total[(i + 1) * rows : (i + 2) * rows].astype(jnp.bfloat16)


def finish_kernel(resid_ref, *refs):
    *mixture_refs, out_ref = refs
    width = mixture_refs[0].shape[1]
    sub = lax.axis_index("sub")
    for bits, mixture_ref in enumerate(mixture_refs):
        lanes = pl.ds(pl.multiple_of((sub ^ bits) * width, 128), width)
        mixture = mixture_ref[...].astype(jnp.float32)
        out_ref[:, lanes] = (resid_ref[:, lanes].astype(jnp.float32) + mixture).astype(jnp.bfloat16)


def flip(x, axis, bits):
    return lax.ppermute(x, axis, [(i, i ^ bits) for i in range(lax.axis_size(axis))])


def per_device(
    tokens,
    queries,
    request_key_cache,
    request_value_cache,
    lengths,
    norm_gain,
    router_weight,
    routes,
    gate_weight,
    up_weight,
    down_weight,
):
    rows, width = tokens.shape
    devs, subs = lax.axis_size("dev"), lax.axis_size("sub")
    all_rows = rows * devs * subs
    cap = 5 * rows * subs // 6
    slots = devs * cap
    own_hidden = gate_weight.shape[1]
    out_width = down_weight.shape[1]
    bf16 = jnp.bfloat16
    opening = call(
        opening_kernel,
        jax.ShapeDtypeStruct((8, 128), jnp.float32),
        (),
        [],
        flops=OPENING_FLOPS,
        vmem=MIB,
    )
    operands = (
        opening,
        lengths,
        routes.T,
        queries,
        request_key_cache,
        request_value_cache,
        tokens,
        norm_gain,
    )
    payload, resid = call(
        attention_kernel,
        (
            jax.ShapeDtypeStruct((rows, width + EXTRA), bf16),
            jax.ShapeDtypeStruct((rows, width), bf16),
        ),
        operands,
        [VMEM_SPEC, SMEM_SPEC, SMEM_SPEC] + [VMEM_SPEC] * 5,
        flops=ATTENTION_FLOPS,
        bytes_accessed=100 * MIB,
        vmem=8 * MIB,
        scratch=[pltpu.VMEM((rows, width), jnp.float32)],
    )
    over_z = [payload] + [flip(payload, "dev", k) for k in range(1, devs)]
    over_x = [flip(p, "sub", 2) for p in over_z]
    pieces = [[z, flip(z, "sub", 1), x, flip(x, "sub", 1)] for z, x in zip(over_z, over_x, strict=True)]
    unit = own_hidden // 16
    widths = [unit * n for n in CHUNKS]
    begins = [sum(widths[:i]) for i in range(len(widths))]
    chunks = len(widths)
    early = [p for k in EARLY for p in pieces[k]]
    block_rows = all_rows // devs
    early_rows = block_rows * len(EARLY)
    packed, extra_early = call(
        functools.partial(pack_kernel, len(early), EARLY, cap),
        (
            jax.ShapeDtypeStruct((slots, width), bf16),
            jax.ShapeDtypeStruct((early_rows, EXTRA), bf16),
        ),
        early,
        [VMEM_SPEC] * len(early),
        flops=PACK_FLOPS,
        vmem=6 * MIB,
        scratch=[pltpu.VMEM((early_rows, width + EXTRA), bf16)],
    )
    late = [p for k in LATE for p in pieces[k]]
    late_rows = block_rows * len(LATE)
    x, extra_late, hidden = call(
        functools.partial(first_hidden_kernel, len(late), LATE, cap),
        (
            jax.ShapeDtypeStruct((slots, width), bf16),
            jax.ShapeDtypeStruct((late_rows, EXTRA), bf16),
            jax.ShapeDtypeStruct((slots, widths[0]), bf16),
        ),
        (*late, packed, gate_weight, up_weight),
        [VMEM_SPEC] * (len(late) + 3),
        flops=GATE_FLOPS,
        vmem=6 * MIB,
        scratch=[pltpu.VMEM((late_rows, width + EXTRA), bf16)],
    )
    own = [hidden]
    for i in range(1, chunks):
        own.append(
            call(
                functools.partial(next_hidden_kernel, begins[i]),
                jax.ShapeDtypeStruct((slots, widths[i]), bf16),
                (x, gate_weight, up_weight),
                [VMEM_SPEC] * 3,
                flops=GATE_FLOPS,
                vmem=4 * MIB,
            )
        )
    far = [flip(h, "sub", 2) for h in own]
    spread, share = call(
        functools.partial(return_kernel, rows, (*EARLY, *LATE), cap),
        (
            jax.ShapeDtypeStruct((all_rows, EXTRA), bf16),
            jax.ShapeDtypeStruct((slots, EXTRA), jnp.float32),
        ),
        (extra_early, extra_late, x, router_weight.T),
        [VMEM_SPEC] * 4,
        flops=DOWN_FLOPS,
        vmem=4 * MIB,
    )
    total_shape = jax.ShapeDtypeStruct((slots, out_width), jnp.float32)
    total = None
    for i in range(chunks):
        wide = widths[i]
        if i < PAIRED:
            both = call(
                pair_kernel,
                jax.ShapeDtypeStruct((slots, 2 * wide), bf16),
                (own[i], far[i]),
                [VMEM_SPEC] * 2,
                flops=10**6,
                vmem=4 * MIB,
            )
            taken = [both, flip(both, "sub", 1)]
            sources = [(0, wide, wide, 2, begins[i]), (1, 0, wide, 1, begins[i]),
                       (1, wide, wide, 3, begins[i])]
        else:
            taken = [far[i], flip(own[i], "sub", 1), flip(far[i], "sub", 1)]
            sources = [(n, 0, wide, bits, begins[i]) for n, bits in enumerate((2, 1, 3))]
        mine = [i] if i < chunks - 2 else [i, i + 1] if i == chunks - 2 else []
        for n in mine:
            sources.append((len(taken), 0, widths[n], 0, begins[n]))
            taken.append(own[n])
        before = () if total is None else (total,)
        if i < chunks - 1:
            total = call(
                functools.partial(down_kernel, sources, own_hidden, i > 0),
                total_shape,
                (*taken, down_weight, *before),
                [VMEM_SPEC] * (len(taken) + 1 + len(before)),
                flops=LAST_FLOPS if i == chunks - 2 else DOWN_FLOPS,
                vmem=4 * MIB,
            )
        else:
            weighted = call(
                functools.partial(last_down_kernel, sources, len(taken), own_hidden),
                (jax.ShapeDtypeStruct((all_rows // devs, out_width), bf16),) * devs,
                (*taken, down_weight, total, spread, share),
                [VMEM_SPEC] * (len(taken) + 4),
                flops=DOWN_FLOPS,
                vmem=4 * MIB,
            )
    weighted = dict(zip((*EARLY, *LATE), weighted, strict=True))
    arrived = [weighted[0]] + [flip(weighted[k], "dev", k) for k in Z_ORDER]
    mixed, to_near, to_far, to_across = call(
        functools.partial(collect_kernel, rows),
        (jax.ShapeDtypeStruct((rows, out_width), jnp.float32),)
        + (jax.ShapeDtypeStruct((rows, out_width), bf16),) * 3,
        arrived,
        [VMEM_SPEC] * devs,
        flops=10**6,
        vmem=4 * MIB,
    )
    from_across = flip(flip(to_across, "sub", 1), "sub", 2)
    from_near = flip(to_near, "sub", 1)
    from_far = flip(to_far, "sub", 2)
    return call(
        finish_kernel,
        jax.ShapeDtypeStruct((rows, width), bf16),
        (resid, mixed, from_near, from_far, from_across),
        [VMEM_SPEC] * 5,
        flops=10**6,
        vmem=4 * MIB,
    )


def solution(mesh):
    in_specs = (
        P(("rep", "dev", "sub"), None),
        P(("rep", "dev", "sub"), None),
        P(("rep", "dev", "sub"), None, None),
        P(("rep", "dev", "sub"), None, None),
        P(("rep", "dev", "sub")),
        P(),
        P(),
        P(("rep", "dev"), None),
        P(None, ("dev", "sub")),
        P(None, ("dev", "sub")),
        P("dev", "sub"),
    )
    out_specs = P(("rep", "dev", "sub"), None)
    one_expert_each = mesh.shape["dev"] == EXPERTS and mesh.shape["sub"] == 4
    return jax.shard_map(
        per_device if one_expert_each else general_plan,
        mesh=mesh,
        in_specs=in_specs,
        out_specs=out_specs,
        check_vma=False,
    )
```

```python
import functools
import math

import jax
import jax.numpy as jnp
from jax import lax
from jax.experimental import pallas as pl
from jax.experimental.pallas import tpu as pltpu
from jax.sharding import PartitionSpec as P

HEAD_SIZE = 128
QUERY_HEADS = 24
KEY_VALUE_HEADS = 4
EXPERTS = 4


def general_plan(
    tokens,
    queries,
    request_key_cache,
    request_value_cache,
    lengths,
    norm_gain,
    router_weight,
    routes,
    gate_weight,
    up_weight,
    down_weight,
):
    token_count = tokens.shape[0]
    feat_width = tokens.shape[1]
    cache_length = request_key_cache.shape[1]
    device_group = QUERY_HEADS // KEY_VALUE_HEADS
    query_tensor_four = queries.reshape(token_count, KEY_VALUE_HEADS, device_group, HEAD_SIZE)
    key_tensor_four = request_key_cache.reshape(
        token_count, cache_length, KEY_VALUE_HEADS, HEAD_SIZE
    )
    value_tensor_four = request_value_cache.reshape(
        token_count, cache_length, KEY_VALUE_HEADS, HEAD_SIZE
    )
    scores = jnp.einsum(
        "thgd,tchd->thgc", query_tensor_four, key_tensor_four, preferred_element_type=jnp.float32
    ) * (1.0 / math.sqrt(HEAD_SIZE))
    in_cache = (jnp.arange(cache_length)[None, :] < lengths[:, None])[:, None, None, :]
    scores = jnp.where(in_cache, scores, -jnp.inf)
    peak_score = jnp.max(scores, axis=-1, keepdims=True)
    exp_scores = jnp.exp(scores - peak_score)
    weights_bf = (exp_scores / jnp.sum(exp_scores, axis=-1, keepdims=True)).astype(jnp.bfloat16)
    attended = jnp.einsum(
        "thgc,tchd->thgd", weights_bf, value_tensor_four, preferred_element_type=jnp.float32
    ).reshape(token_count, feat_width)
    resid = (tokens.astype(jnp.float32) + attended).astype(jnp.bfloat16)
    resid_f = resid.astype(jnp.float32)
    stats = jnp.mean(resid_f * resid_f, axis=-1, keepdims=True)
    normed = (resid_f * lax.rsqrt(stats + 1e-05) * norm_gain.astype(jnp.float32)).astype(
        jnp.bfloat16
    )
    logits = jnp.dot(normed, router_weight, preferred_element_type=jnp.float32)
    sub_index = lax.axis_index("sub")
    sub_count = lax.axis_size("sub")
    dev_count = lax.axis_size("dev")
    expert_ids = jnp.arange(EXPERTS)
    own_routes = lax.dynamic_slice_in_dim(routes, sub_index * token_count, token_count, 0)
    first_logit = jnp.sum(jnp.where(own_routes[:, 0:1] == expert_ids[None, :], logits, 0.0), axis=1)
    second_logit = jnp.sum(
        jnp.where(own_routes[:, 1:2] == expert_ids[None, :], logits, 0.0), axis=1
    )
    first_share = jax.nn.sigmoid(first_logit - second_logit)
    second_share = jax.nn.sigmoid(second_logit - first_logit)
    block_rows = lax.all_gather(normed, "sub", axis=0, tiled=True)
    block_len = token_count * sub_count
    capacity = 5 * block_len // 6
    group_size = dev_count // EXPERTS
    flat_ids = routes.reshape(-1)
    route_hot = (flat_ids[:, None] == expert_ids[None, :]).astype(jnp.int32)
    earlier = jnp.cumsum(route_hot, axis=0) - route_hot
    slot_number = jnp.sum(earlier * route_hot, axis=1)
    slot_index = (flat_ids * capacity + slot_number).reshape(block_len, 2)
    slot_range = jnp.arange(EXPERTS * capacity)
    place_matrix = jnp.any(slot_index[None, :, :] == slot_range[:, None, None], axis=-1).astype(
        jnp.bfloat16
    )
    slot_total = dev_count * capacity
    packed = jnp.dot(place_matrix, block_rows, preferred_element_type=jnp.float32).astype(
        jnp.bfloat16
    )
    outgoing = jnp.repeat(packed.reshape(EXPERTS, capacity, feat_width), group_size, axis=0)
    arrived = lax.all_to_all(outgoing, "dev", split_axis=0, concat_axis=0, tiled=True).reshape(
        slot_total, feat_width
    )
    gate_part = jnp.dot(arrived, gate_weight, preferred_element_type=jnp.float32)
    up_part = jnp.dot(arrived, up_weight, preferred_element_type=jnp.float32)
    hidden = (jax.nn.silu(gate_part) * up_part).astype(jnp.bfloat16)
    out_width = down_weight.shape[1]
    partial_out = jnp.dot(
        lax.all_gather(hidden, "sub", axis=1, tiled=True),
        down_weight,
        preferred_element_type=jnp.float32,
    )
    returned = lax.all_to_all(
        partial_out.reshape(dev_count, capacity, out_width),
        "dev",
        split_axis=0,
        concat_axis=0,
        tiled=True,
    )
    expert_out = jnp.sum(
        returned.reshape(EXPERTS, group_size, capacity, out_width), axis=1
    ).reshape(EXPERTS * capacity, out_width)
    pick_matrix = (slot_index.reshape(-1)[:, None] == slot_range[None, :]).astype(jnp.float32)
    per_route = jnp.dot(pick_matrix, expert_out, precision=lax.Precision.HIGHEST).reshape(
        block_len, 2, out_width
    )
    own_outputs = lax.all_to_all(per_route, "sub", split_axis=0, concat_axis=2, tiled=True)
    mixture = (
        first_share[:, None] * own_outputs[:, 0, :] + second_share[:, None] * own_outputs[:, 1, :]
    )
    return (resid_f + mixture).astype(jnp.bfloat16)


VMEM_SPEC = pl.BlockSpec(memory_space=pltpu.VMEM)
SMEM_SPEC = pl.BlockSpec(memory_space=pltpu.SMEM)
MIB = 1024 * 1024
CHUNKS = (4, 4, 4, 4)
Z_ORDER = (3, 2, 1)
EARLY, LATE = (1, 3), (0, 2)
PAIRED = 0
LAST_FLOPS = 10**9
PACK_FLOPS = 10**8
OPENING_FLOPS = 6 * 10**9
ATTENTION_FLOPS = 30 * 10**9
GATE_FLOPS = 10**9
DOWN_FLOPS = 10**9
EXTRA = 128


def call(body, out_shapes, operands, specs, flops, vmem, scratch=(), bytes_accessed=0):
    return pl.pallas_call(
        body,
        out_shape=out_shapes,
        in_specs=specs,
        out_specs=jax.tree.map(lambda _: VMEM_SPEC, out_shapes),
        scratch_shapes=list(scratch),
        compiler_params=pltpu.CompilerParams(vmem_limit_bytes=vmem),
        cost_estimate=pl.CostEstimate(
            flops=flops, bytes_accessed=bytes_accessed, transcendentals=0
        ),
    )(*operands)


def dot(a, b):
    return jnp.dot(a, b, preferred_element_type=jnp.float32)


def dot_nt(a, b):
    return lax.dot_general(a, b, (((1,), (1,)), ((), ())), preferred_element_type=jnp.float32)


def opening_kernel(out_ref):
    out_ref[...] = jnp.zeros_like(out_ref)


def attention_kernel(
    _,
    lengths_ref,
    routes_ref,
    queries_ref,
    keys_ref,
    values_ref,
    tokens_ref,
    gain_ref,
    payload_ref,
    resid_ref,
    att_ref,
):
    rows, width = tokens_ref.shape
    cache = keys_ref.shape[1]
    group = QUERY_HEADS // KEY_VALUE_HEADS
    row = lax.broadcasted_iota(jnp.int32, (rows, 1), 0)
    live = jnp.zeros((rows, 1), jnp.int32)
    first = jnp.zeros((rows, 1), jnp.int32)
    second = jnp.zeros((rows, 1), jnp.int32)
    base = lax.axis_index("sub") * rows
    for t in range(rows):
        live = jnp.where(row == t, lengths_ref[t], live)
        first = jnp.where(row == t, routes_ref[0, base + t], first)
        second = jnp.where(row == t, routes_ref[1, base + t], second)
    column = lax.broadcasted_iota(jnp.int32, (rows, rows * cache), 1)
    start = row * cache
    in_cache = (column >= start) & (column < start + live)
    bias = jnp.where(in_cache, 0.0, -jnp.inf)[None]
    scale = 1.0 / math.sqrt(HEAD_SIZE)
    pair = 4
    for kv in range(0, KEY_VALUE_HEADS, pair):
        lanes = slice(kv * HEAD_SIZE, (kv + pair) * HEAD_SIZE)
        key = keys_ref[:, :, lanes].reshape(rows * cache, pair * HEAD_SIZE)
        value = values_ref[:, :, lanes].reshape(rows * cache, pair * HEAD_SIZE)
        queries = []
        blank = jnp.zeros((group * rows, HEAD_SIZE), jnp.float32)
        for one in range(pair):
            heads = [
                queries_ref[:, h * HEAD_SIZE : (h + 1) * HEAD_SIZE].astype(jnp.float32)
                for h in range((kv + one) * group, (kv + one + 1) * group)
            ]
            blocks = [blank] * pair
            blocks[one] = jnp.concatenate(heads, axis=0)
            queries.append(jnp.concatenate(blocks, axis=1))
        query = jnp.concatenate(queries, axis=0).astype(jnp.bfloat16)
        scores = dot_nt(query, key).reshape(pair * group, rows, rows * cache) * scale + bias
        exp_scores = jnp.exp(scores - jnp.max(scores, axis=2, keepdims=True))
        total = jnp.sum(exp_scores, axis=2, keepdims=True)
        probs = (exp_scores * (1.0 / total)).reshape(pair * group * rows, rows * cache)
        attended = dot(probs.astype(jnp.bfloat16), value)
        for n in range(pair * group):
            h = kv * group + n
            one = n // group
            att_ref[:, h * HEAD_SIZE : (h + 1) * HEAD_SIZE] = attended[
                n * rows : (n + 1) * rows, one * HEAD_SIZE : (one + 1) * HEAD_SIZE
            ]
    resid = (tokens_ref[...].astype(jnp.float32) + att_ref[...]).astype(jnp.bfloat16)
    resid_ref[...] = resid
    resid_f = resid.astype(jnp.float32)
    stats = jnp.sum(resid_f * resid_f, axis=1, keepdims=True) * (1.0 / width)
    gain = gain_ref[...].astype(jnp.float32).reshape(1, width)
    normed = (resid_f * lax.rsqrt(stats + 1e-05) * gain).astype(jnp.bfloat16)
    payload_ref[:, :width] = normed
    lane = lax.broadcasted_iota(jnp.int32, (rows, EXTRA), 1)
    routed = ((first == lane) | (second == lane)).astype(jnp.float32)
    payload_ref[:, width:] = routed.astype(jnp.bfloat16)


def own_offset(rows):
    return lax.axis_index("sub") * rows


def slot_matrix(extra, offset, block_rows, blocks, cap):
    count = extra.shape[0]
    here = lax.broadcasted_iota(jnp.int32, (count, count), 0)
    there = lax.broadcasted_iota(jnp.int32, (count, count), 1)
    before = (there // block_rows == here // block_rows) & ((there ^ offset) < (here ^ offset))
    earlier = dot(before.astype(jnp.bfloat16), extra)
    lane = lax.broadcasted_iota(jnp.int32, (count, EXTRA), 1)
    mine = lane == lax.axis_index("dev")
    rank = jnp.sum(jnp.where(mine, earlier, 0.0), axis=1, keepdims=True)
    routed = jnp.sum(jnp.where(mine, extra.astype(jnp.float32), 0.0), axis=1, keepdims=True)
    block = lax.broadcasted_iota(jnp.int32, (count, 1), 0) // block_rows
    base = jnp.zeros((count, 1), jnp.int32)
    for i, k in enumerate(blocks):
        base = jnp.where(block == i, k * cap, base)
    slot = jnp.where(routed > 0.5, rank.astype(jnp.int32) + base, -1)
    return (slot == lax.broadcasted_iota(jnp.int32, (count, EXTRA), 1)).astype(jnp.float32)


def hidden_columns(x, gate_ref, up_ref, out_ref, begin):
    step = min(256, out_ref.shape[1])
    end = out_ref.shape[1]
    for j in range(0, end, step):
        columns = slice(begin + j, begin + min(j + step, end))
        gate = dot(x, gate_ref[:, columns])
        up = dot(x, up_ref[:, columns])
        out_ref[:, j : min(j + step, end)] = (gate / (1.0 + jnp.exp(-gate)) * up).astype(jnp.bfloat16)


def join(piece_refs, rows_ref):
    at = 0
    for first, second in zip(piece_refs[0::2], piece_refs[1::2], strict=True):
        both = [first[...].astype(jnp.float32), second[...].astype(jnp.float32)]
        size = first.shape[0] + second.shape[0]
        rows_ref[at : at + size, :] = jnp.concatenate(both, axis=0).astype(jnp.bfloat16)
        at += size


def placed(rows_ref, width, piece_rows, blocks, cap, slots):
    block_rows = rows_ref.shape[0] // len(blocks)
    place = slot_matrix(rows_ref[:, width:], own_offset(piece_rows), block_rows, blocks, cap)
    return dot(place.T[:slots].astype(jnp.bfloat16), rows_ref[:, :width])


def pack_kernel(pieces, blocks, cap, *refs):
    x_ref, extra_ref, rows_ref = refs[pieces:]
    slots, width = x_ref.shape
    join(refs[:pieces], rows_ref)
    extra_ref[...] = rows_ref[:, width:]
    x_ref[...] = placed(rows_ref, width, refs[0].shape[0], blocks, cap, slots).astype(jnp.bfloat16)


def first_hidden_kernel(pieces, blocks, cap, *refs):
    packed_ref, gate_ref, up_ref, x_ref, extra_ref, hidden_ref, rows_ref = refs[pieces:]
    slots, width = x_ref.shape
    join(refs[:pieces], rows_ref)
    extra_ref[...] = rows_ref[:, width:]
    late = placed(rows_ref, width, refs[0].shape[0], blocks, cap, slots)
    x_ref[...] = (packed_ref[...].astype(jnp.float32) + late).astype(jnp.bfloat16)
    hidden_columns(x_ref[...], gate_ref, up_ref, hidden_ref, 0)


def next_hidden_kernel(begin, x_ref, gate_ref, up_ref, hidden_ref):
    hidden_columns(x_ref[...], gate_ref, up_ref, hidden_ref, begin)


def pair_kernel(first_ref, second_ref, out_ref):
    width = first_ref.shape[1]
    out_ref[:, :width] = first_ref[...]
    out_ref[:, width:] = second_ref[...]


def down_part(refs, sources, down_ref, own_width):
    sub = lax.axis_index("sub")
    total = None
    for which, start, width, bits, begin in sources:
        at = pl.multiple_of((sub ^ bits) * own_width + begin, 128)
        part = dot(refs[which][:, start : start + width], down_ref[pl.ds(at, width), :])
        total = part if total is None else total + part
    return total


def down_kernel(sources, own_width, has_total, *refs):
    rest = refs[-3:] if has_total else refs[-2:]
    total = down_part(refs, sources, rest[0], own_width)
    if has_total:
        total = total + rest[1][...]
    rest[-1][...] = total


def return_kernel(rows, order, cap, *refs):
    *extra_refs, x_ref, router_ref, spread_ref, share_ref = refs
    slots = share_ref.shape[0]
    extra = jnp.concatenate([ref[...] for ref in extra_refs], axis=0)
    here = slot_matrix(extra, own_offset(rows), extra.shape[0] // len(order), order, cap)
    spread_ref[...] = here.astype(jnp.bfloat16)
    routed = dot(here.T[:slots].astype(jnp.bfloat16), extra)[:, :EXPERTS] > 0.5
    logits = dot_nt(x_ref[...], router_ref[...])
    mine = lax.broadcasted_iota(jnp.int32, logits.shape, 1) == lax.axis_index("dev")
    own_logit = jnp.sum(jnp.where(mine, logits, 0.0), axis=1, keepdims=True)
    other_logit = jnp.sum(jnp.where(routed & ~mine, logits, 0.0), axis=1, keepdims=True)
    share = 1.0 / (1.0 + jnp.exp(other_logit - own_logit))
    share_ref[...] = jnp.broadcast_to(share, share_ref.shape)


def last_down_kernel(sources, operands, own_width, *refs):
    down_ref, total_ref, spread_ref, share_ref, *out_refs = refs[operands:]
    slots = total_ref.shape[0]
    total = total_ref[...] + down_part(refs, sources, down_ref, own_width)
    weighted = (total * share_ref[:, :1]).astype(jnp.bfloat16)
    result = dot(spread_ref[:, :slots], weighted).astype(jnp.bfloat16)
    height = out_refs[0].shape[0]
    for k, out_ref in enumerate(out_refs):
        out_ref[...] = result[k * height : (k + 1) * height]


def collect_kernel(rows, *refs):
    parts, (own_ref, *out_refs) = refs[:-4], refs[-4:]
    total = parts[0][...].astype(jnp.float32)
    for part in parts[1:]:
        total = total + part[...].astype(jnp.float32)
    own_ref[...] = total[:rows]
    for i, out_ref in enumerate(out_refs):
        out_ref[...] = total[(i + 1) * rows : (i + 2) * rows].astype(jnp.bfloat16)


def finish_kernel(resid_ref, *refs):
    *mixture_refs, out_ref = refs
    width = mixture_refs[0].shape[1]
    sub = lax.axis_index("sub")
    for bits, mixture_ref in enumerate(mixture_refs):
        lanes = pl.ds(pl.multiple_of((sub ^ bits) * width, 128), width)
        mixture = mixture_ref[...].astype(jnp.float32)
        out_ref[:, lanes] = (resid_ref[:, lanes].astype(jnp.float32) + mixture).astype(jnp.bfloat16)


def flip(x, axis, bits):
    return lax.ppermute(x, axis, [(i, i ^ bits) for i in range(lax.axis_size(axis))])


def per_device(
    tokens,
    queries,
    request_key_cache,
    request_value_cache,
    lengths,
    norm_gain,
    router_weight,
    routes,
    gate_weight,
    up_weight,
    down_weight,
):
    rows, width = tokens.shape
    devs, subs = lax.axis_size("dev"), lax.axis_size("sub")
    all_rows = rows * devs * subs
    cap = 5 * rows * subs // 6
    slots = devs * cap
    own_hidden = gate_weight.shape[1]
    out_width = down_weight.shape[1]
    bf16 = jnp.bfloat16
    opening = call(
        opening_kernel,
        jax.ShapeDtypeStruct((8, 128), jnp.float32),
        (),
        [],
        flops=OPENING_FLOPS,
        vmem=MIB,
    )
    operands = (
        opening,
        lengths,
        routes.T,
        queries,
        request_key_cache,
        request_value_cache,
        tokens,
        norm_gain,
    )
    payload, resid = call(
        attention_kernel,
        (
            jax.ShapeDtypeStruct((rows, width + EXTRA), bf16),
            jax.ShapeDtypeStruct((rows, width), bf16),
        ),
        operands,
        [VMEM_SPEC, SMEM_SPEC, SMEM_SPEC] + [VMEM_SPEC] * 5,
        flops=ATTENTION_FLOPS,
        bytes_accessed=100 * MIB,
        vmem=8 * MIB,
        scratch=[pltpu.VMEM((rows, width), jnp.float32)],
    )
    over_z = [payload] + [flip(payload, "dev", k) for k in range(1, devs)]
    over_x = [flip(p, "sub", 2) for p in over_z]
    pieces = [[z, flip(z, "sub", 1), x, flip(x, "sub", 1)] for z, x in zip(over_z, over_x, strict=True)]
    unit = own_hidden // 16
    widths = [unit * n for n in CHUNKS]
    begins = [sum(widths[:i]) for i in range(len(widths))]
    chunks = len(widths)
    early = [p for k in EARLY for p in pieces[k]]
    block_rows = all_rows // devs
    early_rows = block_rows * len(EARLY)
    packed, extra_early = call(
        functools.partial(pack_kernel, len(early), EARLY, cap),
        (
            jax.ShapeDtypeStruct((slots, width), bf16),
            jax.ShapeDtypeStruct((early_rows, EXTRA), bf16),
        ),
        early,
        [VMEM_SPEC] * len(early),
        flops=PACK_FLOPS,
        vmem=6 * MIB,
        scratch=[pltpu.VMEM((early_rows, width + EXTRA), bf16)],
    )
    late = [p for k in LATE for p in pieces[k]]
    late_rows = block_rows * len(LATE)
    x, extra_late, hidden = call(
        functools.partial(first_hidden_kernel, len(late), LATE, cap),
        (
            jax.ShapeDtypeStruct((slots, width), bf16),
            jax.ShapeDtypeStruct((late_rows, EXTRA), bf16),
            jax.ShapeDtypeStruct((slots, widths[0]), bf16),
        ),
        (*late, packed, gate_weight, up_weight),
        [VMEM_SPEC] * (len(late) + 3),
        flops=GATE_FLOPS,
        vmem=6 * MIB,
        scratch=[pltpu.VMEM((late_rows, width + EXTRA), bf16)],
    )
    own = [hidden]
    for i in range(1, chunks):
        own.append(
            call(
                functools.partial(next_hidden_kernel, begins[i]),
                jax.ShapeDtypeStruct((slots, widths[i]), bf16),
                (x, gate_weight, up_weight),
                [VMEM_SPEC] * 3,
                flops=GATE_FLOPS,
                vmem=4 * MIB,
            )
        )
    far = [flip(h, "sub", 2) for h in own]
    spread, share = call(
        functools.partial(return_kernel, rows, (*EARLY, *LATE), cap),
        (
            jax.ShapeDtypeStruct((all_rows, EXTRA), bf16),
            jax.ShapeDtypeStruct((slots, EXTRA), jnp.float32),
        ),
        (extra_early, extra_late, x, router_weight.T),
        [VMEM_SPEC] * 4,
        flops=DOWN_FLOPS,
        vmem=4 * MIB,
    )
    total_shape = jax.ShapeDtypeStruct((slots, out_width), jnp.float32)
    total = None
    for i in range(chunks):
        wide = widths[i]
        if i < PAIRED:
            both = call(
                pair_kernel,
                jax.ShapeDtypeStruct((slots, 2 * wide), bf16),
                (own[i], far[i]),
                [VMEM_SPEC] * 2,
                flops=10**6,
                vmem=4 * MIB,
            )
            taken = [both, flip(both, "sub", 1)]
            sources = [(0, wide, wide, 2, begins[i]), (1, 0, wide, 1, begins[i]),
                       (1, wide, wide, 3, begins[i])]
        else:
            taken = [far[i], flip(own[i], "sub", 1), flip(far[i], "sub", 1)]
            sources = [(n, 0, wide, bits, begins[i]) for n, bits in enumerate((2, 1, 3))]
        mine = [i] if i < chunks - 2 else [i, i + 1] if i == chunks - 2 else []
        for n in mine:
            sources.append((len(taken), 0, widths[n], 0, begins[n]))
            taken.append(own[n])
        before = () if total is None else (total,)
        if i < chunks - 1:
            total = call(
                functools.partial(down_kernel, sources, own_hidden, i > 0),
                total_shape,
                (*taken, down_weight, *before),
                [VMEM_SPEC] * (len(taken) + 1 + len(before)),
                flops=LAST_FLOPS if i == chunks - 2 else DOWN_FLOPS,
                vmem=4 * MIB,
            )
        else:
            weighted = call(
                functools.partial(last_down_kernel, sources, len(taken), own_hidden),
                (jax.ShapeDtypeStruct((all_rows // devs, out_width), bf16),) * devs,
                (*taken, down_weight, total, spread, share),
                [VMEM_SPEC] * (len(taken) + 4),
                flops=DOWN_FLOPS,
                vmem=4 * MIB,
            )
    weighted = dict(zip((*EARLY, *LATE), weighted, strict=True))
    arrived = [weighted[0]] + [flip(weighted[k], "dev", k) for k in Z_ORDER]
    mixed, to_near, to_far, to_across = call(
        functools.partial(collect_kernel, rows),
        (jax.ShapeDtypeStruct((rows, out_width), jnp.float32),)
        + (jax.ShapeDtypeStruct((rows, out_width), bf16),) * 3,
        arrived,
        [VMEM_SPEC] * devs,
        flops=10**6,
        vmem=4 * MIB,
    )
    from_near = flip(to_near, "sub", 1)
    from_far = flip(to_far, "sub", 2)
    from_across = flip(to_across, "sub", 3)
    return call(
        finish_kernel,
        jax.ShapeDtypeStruct((rows, width), bf16),
        (resid, mixed, from_near, from_far, from_across),
        [VMEM_SPEC] * 5,
        flops=10**6,
        vmem=4 * MIB,
    )


def solution(mesh):
    in_specs = (
        P(("rep", "dev", "sub"), None),
        P(("rep", "dev", "sub"), None),
        P(("rep", "dev", "sub"), None, None),
        P(("rep", "dev", "sub"), None, None),
        P(("rep", "dev", "sub")),
        P(),
        P(),
        P(("rep", "dev"), None),
        P(None, ("dev", "sub")),
        P(None, ("dev", "sub")),
        P("dev", "sub"),
    )
    out_specs = P(("rep", "dev", "sub"), None)
    one_expert_each = mesh.shape["dev"] == EXPERTS and mesh.shape["sub"] == 4
    return jax.shard_map(
        per_device if one_expert_each else general_plan,
        mesh=mesh,
        in_specs=in_specs,
        out_specs=out_specs,
        check_vma=False,
    )
```

```python
import functools
import math

import jax
import jax.numpy as jnp
from jax import lax
from jax.experimental import pallas as pl
from jax.experimental.pallas import tpu as pltpu
from jax.sharding import PartitionSpec as P

HEAD_SIZE = 128
QUERY_HEADS = 24
KEY_VALUE_HEADS = 4
EXPERTS = 4


def general_plan(
    tokens,
    queries,
    request_key_cache,
    request_value_cache,
    lengths,
    norm_gain,
    router_weight,
    routes,
    gate_weight,
    up_weight,
    down_weight,
):
    token_count = tokens.shape[0]
    feat_width = tokens.shape[1]
    cache_length = request_key_cache.shape[1]
    device_group = QUERY_HEADS // KEY_VALUE_HEADS
    query_tensor_four = queries.reshape(token_count, KEY_VALUE_HEADS, device_group, HEAD_SIZE)
    key_tensor_four = request_key_cache.reshape(
        token_count, cache_length, KEY_VALUE_HEADS, HEAD_SIZE
    )
    value_tensor_four = request_value_cache.reshape(
        token_count, cache_length, KEY_VALUE_HEADS, HEAD_SIZE
    )
    scores = jnp.einsum(
        "thgd,tchd->thgc", query_tensor_four, key_tensor_four, preferred_element_type=jnp.float32
    ) * (1.0 / math.sqrt(HEAD_SIZE))
    in_cache = (jnp.arange(cache_length)[None, :] < lengths[:, None])[:, None, None, :]
    scores = jnp.where(in_cache, scores, -jnp.inf)
    peak_score = jnp.max(scores, axis=-1, keepdims=True)
    exp_scores = jnp.exp(scores - peak_score)
    weights_bf = (exp_scores / jnp.sum(exp_scores, axis=-1, keepdims=True)).astype(jnp.bfloat16)
    attended = jnp.einsum(
        "thgc,tchd->thgd", weights_bf, value_tensor_four, preferred_element_type=jnp.float32
    ).reshape(token_count, feat_width)
    resid = (tokens.astype(jnp.float32) + attended).astype(jnp.bfloat16)
    resid_f = resid.astype(jnp.float32)
    stats = jnp.mean(resid_f * resid_f, axis=-1, keepdims=True)
    normed = (resid_f * lax.rsqrt(stats + 1e-05) * norm_gain.astype(jnp.float32)).astype(
        jnp.bfloat16
    )
    logits = jnp.dot(normed, router_weight, preferred_element_type=jnp.float32)
    sub_index = lax.axis_index("sub")
    sub_count = lax.axis_size("sub")
    dev_count = lax.axis_size("dev")
    expert_ids = jnp.arange(EXPERTS)
    own_routes = lax.dynamic_slice_in_dim(routes, sub_index * token_count, token_count, 0)
    first_logit = jnp.sum(jnp.where(own_routes[:, 0:1] == expert_ids[None, :], logits, 0.0), axis=1)
    second_logit = jnp.sum(
        jnp.where(own_routes[:, 1:2] == expert_ids[None, :], logits, 0.0), axis=1
    )
    first_share = jax.nn.sigmoid(first_logit - second_logit)
    second_share = jax.nn.sigmoid(second_logit - first_logit)
    block_rows = lax.all_gather(normed, "sub", axis=0, tiled=True)
    block_len = token_count * sub_count
    capacity = 5 * block_len // 6
    group_size = dev_count // EXPERTS
    flat_ids = routes.reshape(-1)
    route_hot = (flat_ids[:, None] == expert_ids[None, :]).astype(jnp.int32)
    earlier = jnp.cumsum(route_hot, axis=0) - route_hot
    slot_number = jnp.sum(earlier * route_hot, axis=1)
    slot_index = (flat_ids * capacity + slot_number).reshape(block_len, 2)
    slot_range = jnp.arange(EXPERTS * capacity)
    place_matrix = jnp.any(slot_index[None, :, :] == slot_range[:, None, None], axis=-1).astype(
        jnp.bfloat16
    )
    slot_total = dev_count * capacity
    packed = jnp.dot(place_matrix, block_rows, preferred_element_type=jnp.float32).astype(
        jnp.bfloat16
    )
    outgoing = jnp.repeat(packed.reshape(EXPERTS, capacity, feat_width), group_size, axis=0)
    arrived = lax.all_to_all(outgoing, "dev", split_axis=0, concat_axis=0, tiled=True).reshape(
        slot_total, feat_width
    )
    gate_part = jnp.dot(arrived, gate_weight, preferred_element_type=jnp.float32)
    up_part = jnp.dot(arrived, up_weight, preferred_element_type=jnp.float32)
    hidden = (jax.nn.silu(gate_part) * up_part).astype(jnp.bfloat16)
    out_width = down_weight.shape[1]
    partial_out = jnp.dot(
        lax.all_gather(hidden, "sub", axis=1, tiled=True),
        down_weight,
        preferred_element_type=jnp.float32,
    )
    returned = lax.all_to_all(
        partial_out.reshape(dev_count, capacity, out_width),
        "dev",
        split_axis=0,
        concat_axis=0,
        tiled=True,
    )
    expert_out = jnp.sum(
        returned.reshape(EXPERTS, group_size, capacity, out_width), axis=1
    ).reshape(EXPERTS * capacity, out_width)
    pick_matrix = (slot_index.reshape(-1)[:, None] == slot_range[None, :]).astype(jnp.float32)
    per_route = jnp.dot(pick_matrix, expert_out, precision=lax.Precision.HIGHEST).reshape(
        block_len, 2, out_width
    )
    own_outputs = lax.all_to_all(per_route, "sub", split_axis=0, concat_axis=2, tiled=True)
    mixture = (
        first_share[:, None] * own_outputs[:, 0, :] + second_share[:, None] * own_outputs[:, 1, :]
    )
    return (resid_f + mixture).astype(jnp.bfloat16)


VMEM_SPEC = pl.BlockSpec(memory_space=pltpu.VMEM)
SMEM_SPEC = pl.BlockSpec(memory_space=pltpu.SMEM)
MIB = 1024 * 1024
CHUNKS = (4, 4, 4, 4)
Z_ORDER = (3, 2, 1)
EARLY, LATE = (1, 3), (0, 2)
DOWN_GROUPS = ((0,), (1,), (2,), (3,))
PACK_FLOPS = 10**8
OPENING_FLOPS = 6 * 10**9
ATTENTION_FLOPS = 30 * 10**9
GATE_FLOPS = 10**9
DOWN_FLOPS = 10**9
EXTRA = 128


def call(body, out_shapes, operands, specs, flops, vmem, scratch=(), bytes_accessed=0):
    return pl.pallas_call(
        body,
        out_shape=out_shapes,
        in_specs=specs,
        out_specs=jax.tree.map(lambda _: VMEM_SPEC, out_shapes),
        scratch_shapes=list(scratch),
        compiler_params=pltpu.CompilerParams(vmem_limit_bytes=vmem),
        cost_estimate=pl.CostEstimate(
            flops=flops, bytes_accessed=bytes_accessed, transcendentals=0
        ),
    )(*operands)


def dot(a, b):
    return jnp.dot(a, b, preferred_element_type=jnp.float32)


def dot_nt(a, b):
    return lax.dot_general(a, b, (((1,), (1,)), ((), ())), preferred_element_type=jnp.float32)


def opening_kernel(out_ref):
    out_ref[...] = jnp.zeros_like(out_ref)


def attention_kernel(
    _,
    lengths_ref,
    routes_ref,
    queries_ref,
    keys_ref,
    values_ref,
    tokens_ref,
    gain_ref,
    payload_ref,
    resid_ref,
    att_ref,
):
    rows, width = tokens_ref.shape
    cache = keys_ref.shape[1]
    group = QUERY_HEADS // KEY_VALUE_HEADS
    row = lax.broadcasted_iota(jnp.int32, (rows, 1), 0)
    live = jnp.zeros((rows, 1), jnp.int32)
    first = jnp.zeros((rows, 1), jnp.int32)
    second = jnp.zeros((rows, 1), jnp.int32)
    base = lax.axis_index("sub") * rows
    for t in range(rows):
        live = jnp.where(row == t, lengths_ref[t], live)
        first = jnp.where(row == t, routes_ref[0, base + t], first)
        second = jnp.where(row == t, routes_ref[1, base + t], second)
    column = lax.broadcasted_iota(jnp.int32, (rows, rows * cache), 1)
    start = row * cache
    in_cache = (column >= start) & (column < start + live)
    bias = jnp.where(in_cache, 0.0, -jnp.inf)[None]
    scale = 1.0 / math.sqrt(HEAD_SIZE)
    pair = 4
    for kv in range(0, KEY_VALUE_HEADS, pair):
        lanes = slice(kv * HEAD_SIZE, (kv + pair) * HEAD_SIZE)
        key = keys_ref[:, :, lanes].reshape(rows * cache, pair * HEAD_SIZE)
        value = values_ref[:, :, lanes].reshape(rows * cache, pair * HEAD_SIZE)
        queries = []
        blank = jnp.zeros((group * rows, HEAD_SIZE), jnp.float32)
        for one in range(pair):
            heads = [
                queries_ref[:, h * HEAD_SIZE : (h + 1) * HEAD_SIZE].astype(jnp.float32)
                for h in range((kv + one) * group, (kv + one + 1) * group)
            ]
            blocks = [blank] * pair
            blocks[one] = jnp.concatenate(heads, axis=0)
            queries.append(jnp.concatenate(blocks, axis=1))
        query = jnp.concatenate(queries, axis=0).astype(jnp.bfloat16)
        scores = dot_nt(query, key).reshape(pair * group, rows, rows * cache) * scale + bias
        exp_scores = jnp.exp(scores - jnp.max(scores, axis=2, keepdims=True))
        total = jnp.sum(exp_scores, axis=2, keepdims=True)
        probs = (exp_scores * (1.0 / total)).reshape(pair * group * rows, rows * cache)
        attended = dot(probs.astype(jnp.bfloat16), value)
        for n in range(pair * group):
            h = kv * group + n
            one = n // group
            att_ref[:, h * HEAD_SIZE : (h + 1) * HEAD_SIZE] = attended[
                n * rows : (n + 1) * rows, one * HEAD_SIZE : (one + 1) * HEAD_SIZE
            ]
    resid = (tokens_ref[...].astype(jnp.float32) + att_ref[...]).astype(jnp.bfloat16)
    resid_ref[...] = resid
    resid_f = resid.astype(jnp.float32)
    stats = jnp.sum(resid_f * resid_f, axis=1, keepdims=True) * (1.0 / width)
    gain = gain_ref[...].astype(jnp.float32).reshape(1, width)
    normed = (resid_f * lax.rsqrt(stats + 1e-05) * gain).astype(jnp.bfloat16)
    payload_ref[:, :width] = normed
    lane = lax.broadcasted_iota(jnp.int32, (rows, EXTRA), 1)
    routed = ((first == lane) | (second == lane)).astype(jnp.float32)
    payload_ref[:, width:] = routed.astype(jnp.bfloat16)


def own_offset(rows):
    return lax.axis_index("sub") * rows


def slot_matrix(extra, offset, block_rows, blocks, cap):
    count = extra.shape[0]
    here = lax.broadcasted_iota(jnp.int32, (count, count), 0)
    there = lax.broadcasted_iota(jnp.int32, (count, count), 1)
    before = (there // block_rows == here // block_rows) & ((there ^ offset) < (here ^ offset))
    earlier = dot(before.astype(jnp.bfloat16), extra)
    lane = lax.broadcasted_iota(jnp.int32, (count, EXTRA), 1)
    mine = lane == lax.axis_index("dev")
    rank = jnp.sum(jnp.where(mine, earlier, 0.0), axis=1, keepdims=True)
    routed = jnp.sum(jnp.where(mine, extra.astype(jnp.float32), 0.0), axis=1, keepdims=True)
    block = lax.broadcasted_iota(jnp.int32, (count, 1), 0) // block_rows
    base = jnp.zeros((count, 1), jnp.int32)
    for i, k in enumerate(blocks):
        base = jnp.where(block == i, k * cap, base)
    slot = jnp.where(routed > 0.5, rank.astype(jnp.int32) + base, -1)
    return (slot == lax.broadcasted_iota(jnp.int32, (count, EXTRA), 1)).astype(jnp.float32)


def hidden_columns(x, gate_ref, up_ref, out_ref, begin):
    step = min(512, out_ref.shape[1])
    end = out_ref.shape[1]
    for j in range(0, end, step):
        columns = slice(begin + j, begin + min(j + step, end))
        gate = dot(x, gate_ref[:, columns])
        up = dot(x, up_ref[:, columns])
        out_ref[:, j : min(j + step, end)] = (gate / (1.0 + jnp.exp(-gate)) * up).astype(jnp.bfloat16)


def join(piece_refs, rows_ref):
    at = 0
    for first, second in zip(piece_refs[0::2], piece_refs[1::2], strict=True):
        both = [first[...].astype(jnp.float32), second[...].astype(jnp.float32)]
        size = first.shape[0] + second.shape[0]
        rows_ref[at : at + size, :] = jnp.concatenate(both, axis=0).astype(jnp.bfloat16)
        at += size


def placed(rows_ref, width, piece_rows, blocks, cap, slots):
    block_rows = rows_ref.shape[0] // len(blocks)
    place = slot_matrix(rows_ref[:, width:], own_offset(piece_rows), block_rows, blocks, cap)
    return dot(place.T[:slots].astype(jnp.bfloat16), rows_ref[:, :width])


def pack_kernel(pieces, blocks, cap, *refs):
    x_ref, extra_ref, rows_ref = refs[pieces:]
    slots, width = x_ref.shape
    join(refs[:pieces], rows_ref)
    extra_ref[...] = rows_ref[:, width:]
    x_ref[...] = placed(rows_ref, width, refs[0].shape[0], blocks, cap, slots).astype(jnp.bfloat16)


def first_hidden_kernel(pieces, blocks, cap, *refs):
    packed_ref, gate_ref, up_ref, x_ref, extra_ref, hidden_ref, rows_ref = refs[pieces:]
    slots, width = x_ref.shape
    join(refs[:pieces], rows_ref)
    extra_ref[...] = rows_ref[:, width:]
    late = placed(rows_ref, width, refs[0].shape[0], blocks, cap, slots)
    x_ref[...] = (packed_ref[...].astype(jnp.float32) + late).astype(jnp.bfloat16)
    hidden_columns(x_ref[...], gate_ref, up_ref, hidden_ref, 0)


def next_hidden_kernel(begin, x_ref, gate_ref, up_ref, hidden_ref):
    hidden_columns(x_ref[...], gate_ref, up_ref, hidden_ref, begin)


def down_part(refs, sources, down_ref, own_width):
    sub = lax.axis_index("sub")
    total = None
    for which, start, width, bits, begin in sources:
        at = pl.multiple_of((sub ^ bits) * own_width + begin, 128)
        part = dot(refs[which][:, start : start + width], down_ref[pl.ds(at, width), :])
        total = part if total is None else total + part
    return total


def down_kernel(sources, own_width, has_total, *refs):
    rest = refs[-3:] if has_total else refs[-2:]
    total = down_part(refs, sources, rest[0], own_width)
    if has_total:
        total = total + rest[1][...]
    rest[-1][...] = total


def return_kernel(rows, order, cap, *refs):
    *extra_refs, x_ref, router_ref, spread_ref, share_ref = refs
    slots = share_ref.shape[0]
    extra = jnp.concatenate([ref[...] for ref in extra_refs], axis=0)
    here = slot_matrix(extra, own_offset(rows), extra.shape[0] // len(order), order, cap)
    spread_ref[...] = here.astype(jnp.bfloat16)
    routed = dot(here.T[:slots].astype(jnp.bfloat16), extra)[:, :EXPERTS] > 0.5
    logits = dot_nt(x_ref[...], router_ref[...])
    mine = lax.broadcasted_iota(jnp.int32, logits.shape, 1) == lax.axis_index("dev")
    own_logit = jnp.sum(jnp.where(mine, logits, 0.0), axis=1, keepdims=True)
    other_logit = jnp.sum(jnp.where(routed & ~mine, logits, 0.0), axis=1, keepdims=True)
    share = 1.0 / (1.0 + jnp.exp(other_logit - own_logit))
    share_ref[...] = jnp.broadcast_to(share, share_ref.shape)


def last_down_kernel(sources, operands, own_width, *refs):
    down_ref, total_ref, spread_ref, share_ref, *out_refs = refs[operands:]
    slots = total_ref.shape[0]
    total = total_ref[...] + down_part(refs, sources, down_ref, own_width)
    weighted = (total * share_ref[:, :1]).astype(jnp.bfloat16)
    result = dot(spread_ref[:, :slots], weighted).astype(jnp.bfloat16)
    height = out_refs[0].shape[0]
    for k, out_ref in enumerate(out_refs):
        out_ref[...] = result[k * height : (k + 1) * height]


def collect_kernel(rows, *refs):
    parts, (own_ref, *out_refs) = refs[:-4], refs[-4:]
    total = parts[0][...].astype(jnp.float32)
    for part in parts[1:]:
        total = total + part[...].astype(jnp.float32)
    own_ref[...] = total[:rows]
    for i, out_ref in enumerate(out_refs):
        out_ref[...] = total[(i + 1) * rows : (i + 2) * rows].astype(jnp.bfloat16)


def finish_kernel(resid_ref, *refs):
    *mixture_refs, out_ref = refs
    width = mixture_refs[0].shape[1]
    sub = lax.axis_index("sub")
    for bits, mixture_ref in enumerate(mixture_refs):
        lanes = pl.ds(pl.multiple_of((sub ^ bits) * width, 128), width)
        mixture = mixture_ref[...].astype(jnp.float32)
        out_ref[:, lanes] = (resid_ref[:, lanes].astype(jnp.float32) + mixture).astype(jnp.bfloat16)


def flip(x, axis, bits):
    return lax.ppermute(x, axis, [(i, i ^ bits) for i in range(lax.axis_size(axis))])


def per_device(
    tokens,
    queries,
    request_key_cache,
    request_value_cache,
    lengths,
    norm_gain,
    router_weight,
    routes,
    gate_weight,
    up_weight,
    down_weight,
):
    rows, width = tokens.shape
    devs, subs = lax.axis_size("dev"), lax.axis_size("sub")
    all_rows = rows * devs * subs
    cap = 5 * rows * subs // 6
    slots = devs * cap
    own_hidden = gate_weight.shape[1]
    out_width = down_weight.shape[1]
    bf16 = jnp.bfloat16
    opening = call(
        opening_kernel,
        jax.ShapeDtypeStruct((8, 128), jnp.float32),
        (),
        [],
        flops=OPENING_FLOPS,
        vmem=MIB,
    )
    operands = (
        opening,
        lengths,
        routes.T,
        queries,
        request_key_cache,
        request_value_cache,
        tokens,
        norm_gain,
    )
    payload, resid = call(
        attention_kernel,
        (
            jax.ShapeDtypeStruct((rows, width + EXTRA), bf16),
            jax.ShapeDtypeStruct((rows, width), bf16),
        ),
        operands,
        [VMEM_SPEC, SMEM_SPEC, SMEM_SPEC] + [VMEM_SPEC] * 5,
        flops=ATTENTION_FLOPS,
        bytes_accessed=100 * MIB,
        vmem=8 * MIB,
        scratch=[pltpu.VMEM((rows, width), jnp.float32)],
    )
    over_z = [payload] + [flip(payload, "dev", k) for k in range(1, devs)]
    over_x = [flip(p, "sub", 2) for p in over_z]
    pieces = [[z, flip(z, "sub", 1), x, flip(x, "sub", 1)] for z, x in zip(over_z, over_x, strict=True)]
    unit = own_hidden // 16
    widths = [unit * n for n in CHUNKS]
    begins = [sum(widths[:i]) for i in range(len(widths))]
    chunks = len(widths)
    early = [p for k in EARLY for p in pieces[k]]
    block_rows = all_rows // devs
    early_rows = block_rows * len(EARLY)
    packed, extra_early = call(
        functools.partial(pack_kernel, len(early), EARLY, cap),
        (
            jax.ShapeDtypeStruct((slots, width), bf16),
            jax.ShapeDtypeStruct((early_rows, EXTRA), bf16),
        ),
        early,
        [VMEM_SPEC] * len(early),
        flops=PACK_FLOPS,
        vmem=6 * MIB,
        scratch=[pltpu.VMEM((early_rows, width + EXTRA), bf16)],
    )
    late = [p for k in LATE for p in pieces[k]]
    late_rows = block_rows * len(LATE)
    x, extra_late, hidden = call(
        functools.partial(first_hidden_kernel, len(late), LATE, cap),
        (
            jax.ShapeDtypeStruct((slots, width), bf16),
            jax.ShapeDtypeStruct((late_rows, EXTRA), bf16),
            jax.ShapeDtypeStruct((slots, widths[0]), bf16),
        ),
        (*late, packed, gate_weight, up_weight),
        [VMEM_SPEC] * (len(late) + 3),
        flops=GATE_FLOPS,
        vmem=6 * MIB,
        scratch=[pltpu.VMEM((late_rows, width + EXTRA), bf16)],
    )
    own = [hidden]
    for i in range(1, chunks):
        own.append(
            call(
                functools.partial(next_hidden_kernel, begins[i]),
                jax.ShapeDtypeStruct((slots, widths[i]), bf16),
                (x, gate_weight, up_weight),
                [VMEM_SPEC] * 3,
                flops=GATE_FLOPS,
                vmem=4 * MIB,
            )
        )
    far = [flip(h, "sub", 2) for h in own]
    spread, share = call(
        functools.partial(return_kernel, rows, (*EARLY, *LATE), cap),
        (
            jax.ShapeDtypeStruct((all_rows, EXTRA), bf16),
            jax.ShapeDtypeStruct((slots, EXTRA), jnp.float32),
        ),
        (extra_early, extra_late, x, router_weight.T),
        [VMEM_SPEC] * 4,
        flops=DOWN_FLOPS,
        vmem=4 * MIB,
    )
    total_shape = jax.ShapeDtypeStruct((slots, out_width), jnp.float32)
    total = None
    for group in DOWN_GROUPS:
        taken, sources = [], []
        for i in group:
            for bits, array in ((2, far[i]), (1, flip(own[i], "sub", 1)), (3, flip(far[i], "sub", 1))):
                sources.append((len(taken), 0, widths[i], bits, begins[i]))
                taken.append(array)
            for n in [i] if i < chunks - 2 else [i, i + 1] if i == chunks - 2 else []:
                sources.append((len(taken), 0, widths[n], 0, begins[n]))
                taken.append(own[n])
        before = () if total is None else (total,)
        if group[-1] < chunks - 1:
            total = call(
                functools.partial(down_kernel, sources, own_hidden, total is not None),
                total_shape,
                (*taken, down_weight, *before),
                [VMEM_SPEC] * (len(taken) + 1 + len(before)),
                flops=DOWN_FLOPS * len(group),
                vmem=4 * MIB,
            )
        else:
            weighted = call(
                functools.partial(last_down_kernel, sources, len(taken), own_hidden),
                (jax.ShapeDtypeStruct((all_rows // devs, out_width), bf16),) * devs,
                (*taken, down_weight, total, spread, share),
                [VMEM_SPEC] * (len(taken) + 4),
                flops=DOWN_FLOPS,
                vmem=4 * MIB,
            )
    weighted = dict(zip((*EARLY, *LATE), weighted, strict=True))
    arrived = [weighted[0]] + [flip(weighted[k], "dev", k) for k in Z_ORDER]
    mixed, to_near, to_far, to_across = call(
        functools.partial(collect_kernel, rows),
        (jax.ShapeDtypeStruct((rows, out_width), jnp.float32),)
        + (jax.ShapeDtypeStruct((rows, out_width), bf16),) * 3,
        arrived,
        [VMEM_SPEC] * devs,
        flops=10**6,
        vmem=4 * MIB,
    )
    from_near = flip(to_near, "sub", 1)
    from_far = flip(to_far, "sub", 2)
    from_across = flip(to_across, "sub", 3)
    return call(
        finish_kernel,
        jax.ShapeDtypeStruct((rows, width), bf16),
        (resid, mixed, from_near, from_far, from_across),
        [VMEM_SPEC] * 5,
        flops=10**6,
        vmem=4 * MIB,
    )


def solution(mesh):
    in_specs = (
        P(("rep", "dev", "sub"), None),
        P(("rep", "dev", "sub"), None),
        P(("rep", "dev", "sub"), None, None),
        P(("rep", "dev", "sub"), None, None),
        P(("rep", "dev", "sub")),
        P(),
        P(),
        P(("rep", "dev"), None),
        P(None, ("dev", "sub")),
        P(None, ("dev", "sub")),
        P("dev", "sub"),
    )
    out_specs = P(("rep", "dev", "sub"), None)
    one_expert_each = mesh.shape["dev"] == EXPERTS and mesh.shape["sub"] == 4
    return jax.shard_map(
        per_device if one_expert_each else general_plan,
        mesh=mesh,
        in_specs=in_specs,
        out_specs=out_specs,
        check_vma=False,
    )
```

```python
import functools
import math

import jax
import jax.numpy as jnp
from jax import lax
from jax.experimental import pallas as pl
from jax.experimental.pallas import tpu as pltpu
from jax.sharding import PartitionSpec as P

HEAD_SIZE = 128
QUERY_HEADS = 24
KEY_VALUE_HEADS = 4
EXPERTS = 4


def general_plan(
    tokens,
    queries,
    request_key_cache,
    request_value_cache,
    lengths,
    norm_gain,
    router_weight,
    routes,
    gate_weight,
    up_weight,
    down_weight,
):
    token_count = tokens.shape[0]
    feat_width = tokens.shape[1]
    cache_length = request_key_cache.shape[1]
    device_group = QUERY_HEADS // KEY_VALUE_HEADS
    query_tensor_four = queries.reshape(token_count, KEY_VALUE_HEADS, device_group, HEAD_SIZE)
    key_tensor_four = request_key_cache.reshape(
        token_count, cache_length, KEY_VALUE_HEADS, HEAD_SIZE
    )
    value_tensor_four = request_value_cache.reshape(
        token_count, cache_length, KEY_VALUE_HEADS, HEAD_SIZE
    )
    scores = jnp.einsum(
        "thgd,tchd->thgc", query_tensor_four, key_tensor_four, preferred_element_type=jnp.float32
    ) * (1.0 / math.sqrt(HEAD_SIZE))
    in_cache = (jnp.arange(cache_length)[None, :] < lengths[:, None])[:, None, None, :]
    scores = jnp.where(in_cache, scores, -jnp.inf)
    peak_score = jnp.max(scores, axis=-1, keepdims=True)
    exp_scores = jnp.exp(scores - peak_score)
    weights_bf = (exp_scores / jnp.sum(exp_scores, axis=-1, keepdims=True)).astype(jnp.bfloat16)
    attended = jnp.einsum(
        "thgc,tchd->thgd", weights_bf, value_tensor_four, preferred_element_type=jnp.float32
    ).reshape(token_count, feat_width)
    resid = (tokens.astype(jnp.float32) + attended).astype(jnp.bfloat16)
    resid_f = resid.astype(jnp.float32)
    stats = jnp.mean(resid_f * resid_f, axis=-1, keepdims=True)
    normed = (resid_f * lax.rsqrt(stats + 1e-05) * norm_gain.astype(jnp.float32)).astype(
        jnp.bfloat16
    )
    logits = jnp.dot(normed, router_weight, preferred_element_type=jnp.float32)
    sub_index = lax.axis_index("sub")
    sub_count = lax.axis_size("sub")
    dev_count = lax.axis_size("dev")
    expert_ids = jnp.arange(EXPERTS)
    own_routes = lax.dynamic_slice_in_dim(routes, sub_index * token_count, token_count, 0)
    first_logit = jnp.sum(jnp.where(own_routes[:, 0:1] == expert_ids[None, :], logits, 0.0), axis=1)
    second_logit = jnp.sum(
        jnp.where(own_routes[:, 1:2] == expert_ids[None, :], logits, 0.0), axis=1
    )
    first_share = jax.nn.sigmoid(first_logit - second_logit)
    second_share = jax.nn.sigmoid(second_logit - first_logit)
    block_rows = lax.all_gather(normed, "sub", axis=0, tiled=True)
    block_len = token_count * sub_count
    capacity = 5 * block_len // 6
    group_size = dev_count // EXPERTS
    flat_ids = routes.reshape(-1)
    route_hot = (flat_ids[:, None] == expert_ids[None, :]).astype(jnp.int32)
    earlier = jnp.cumsum(route_hot, axis=0) - route_hot
    slot_number = jnp.sum(earlier * route_hot, axis=1)
    slot_index = (flat_ids * capacity + slot_number).reshape(block_len, 2)
    slot_range = jnp.arange(EXPERTS * capacity)
    place_matrix = jnp.any(slot_index[None, :, :] == slot_range[:, None, None], axis=-1).astype(
        jnp.bfloat16
    )
    slot_total = dev_count * capacity
    packed = jnp.dot(place_matrix, block_rows, preferred_element_type=jnp.float32).astype(
        jnp.bfloat16
    )
    outgoing = jnp.repeat(packed.reshape(EXPERTS, capacity, feat_width), group_size, axis=0)
    arrived = lax.all_to_all(outgoing, "dev", split_axis=0, concat_axis=0, tiled=True).reshape(
        slot_total, feat_width
    )
    gate_part = jnp.dot(arrived, gate_weight, preferred_element_type=jnp.float32)
    up_part = jnp.dot(arrived, up_weight, preferred_element_type=jnp.float32)
    hidden = (jax.nn.silu(gate_part) * up_part).astype(jnp.bfloat16)
    out_width = down_weight.shape[1]
    partial_out = jnp.dot(
        lax.all_gather(hidden, "sub", axis=1, tiled=True),
        down_weight,
        preferred_element_type=jnp.float32,
    )
    returned = lax.all_to_all(
        partial_out.reshape(dev_count, capacity, out_width),
        "dev",
        split_axis=0,
        concat_axis=0,
        tiled=True,
    )
    expert_out = jnp.sum(
        returned.reshape(EXPERTS, group_size, capacity, out_width), axis=1
    ).reshape(EXPERTS * capacity, out_width)
    pick_matrix = (slot_index.reshape(-1)[:, None] == slot_range[None, :]).astype(jnp.float32)
    per_route = jnp.dot(pick_matrix, expert_out, precision=lax.Precision.HIGHEST).reshape(
        block_len, 2, out_width
    )
    own_outputs = lax.all_to_all(per_route, "sub", split_axis=0, concat_axis=2, tiled=True)
    mixture = (
        first_share[:, None] * own_outputs[:, 0, :] + second_share[:, None] * own_outputs[:, 1, :]
    )
    return (resid_f + mixture).astype(jnp.bfloat16)


VMEM_SPEC = pl.BlockSpec(memory_space=pltpu.VMEM)
SMEM_SPEC = pl.BlockSpec(memory_space=pltpu.SMEM)
MIB = 1024 * 1024
CHUNKS = (4, 4, 4, 4)
Z_ORDER = (3, 2, 1)
EARLY, LATE = (1, 3), (0, 2)
DOWN_GROUPS = ((0,), (1,), (2,), (3,))
PACK_FLOPS = 10**8
OPENING_FLOPS = 6 * 10**9
ATTENTION_FLOPS = 30 * 10**9
GATE_FLOPS = 10**9
DOWN_FLOPS = 10**9
EXTRA = 128


def call(body, out_shapes, operands, specs, flops, vmem, scratch=(), bytes_accessed=0):
    return pl.pallas_call(
        body,
        out_shape=out_shapes,
        in_specs=specs,
        out_specs=jax.tree.map(lambda _: VMEM_SPEC, out_shapes),
        scratch_shapes=list(scratch),
        compiler_params=pltpu.CompilerParams(vmem_limit_bytes=vmem),
        cost_estimate=pl.CostEstimate(
            flops=flops, bytes_accessed=bytes_accessed, transcendentals=0
        ),
    )(*operands)


def dot(a, b):
    return jnp.dot(a, b, preferred_element_type=jnp.float32)


def dot_nt(a, b):
    return lax.dot_general(a, b, (((1,), (1,)), ((), ())), preferred_element_type=jnp.float32)


def opening_kernel(out_ref):
    out_ref[...] = jnp.zeros_like(out_ref)


def attention_kernel(
    _,
    lengths_ref,
    routes_ref,
    queries_ref,
    keys_ref,
    values_ref,
    tokens_ref,
    gain_ref,
    payload_ref,
    resid_ref,
    att_ref,
):
    rows, width = tokens_ref.shape
    cache = keys_ref.shape[1]
    group = QUERY_HEADS // KEY_VALUE_HEADS
    row = lax.broadcasted_iota(jnp.int32, (rows, 1), 0)
    live = jnp.zeros((rows, 1), jnp.int32)
    first = jnp.zeros((rows, 1), jnp.int32)
    second = jnp.zeros((rows, 1), jnp.int32)
    base = lax.axis_index("sub") * rows
    for t in range(rows):
        live = jnp.where(row == t, lengths_ref[t], live)
        first = jnp.where(row == t, routes_ref[0, base + t], first)
        second = jnp.where(row == t, routes_ref[1, base + t], second)
    column = lax.broadcasted_iota(jnp.int32, (rows, rows * cache), 1)
    start = row * cache
    in_cache = (column >= start) & (column < start + live)
    bias = jnp.where(in_cache, 0.0, -jnp.inf)[None]
    scale = 1.0 / math.sqrt(HEAD_SIZE)
    pair = 4
    for kv in range(0, KEY_VALUE_HEADS, pair):
        lanes = slice(kv * HEAD_SIZE, (kv + pair) * HEAD_SIZE)
        key = keys_ref[:, :, lanes].reshape(rows * cache, pair * HEAD_SIZE)
        value = values_ref[:, :, lanes].reshape(rows * cache, pair * HEAD_SIZE)
        queries = []
        blank = jnp.zeros((group * rows, HEAD_SIZE), jnp.float32)
        for one in range(pair):
            heads = [
                queries_ref[:, h * HEAD_SIZE : (h + 1) * HEAD_SIZE].astype(jnp.float32)
                for h in range((kv + one) * group, (kv + one + 1) * group)
            ]
            blocks = [blank] * pair
            blocks[one] = jnp.concatenate(heads, axis=0)
            queries.append(jnp.concatenate(blocks, axis=1))
        query = jnp.concatenate(queries, axis=0).astype(jnp.bfloat16)
        scores = dot_nt(query, key).reshape(pair * group, rows, rows * cache) * scale + bias
        exp_scores = jnp.exp(scores - jnp.max(scores, axis=2, keepdims=True))
        total = jnp.sum(exp_scores, axis=2, keepdims=True)
        weights = exp_scores.reshape(pair * group * rows, rows * cache).astype(jnp.bfloat16)
        attended = dot(weights, value) * (1.0 / total).reshape(pair * group * rows, 1)
        for n in range(pair * group):
            h = kv * group + n
            one = n // group
            att_ref[:, h * HEAD_SIZE : (h + 1) * HEAD_SIZE] = attended[
                n * rows : (n + 1) * rows, one * HEAD_SIZE : (one + 1) * HEAD_SIZE
            ]
    resid = (tokens_ref[...].astype(jnp.float32) + att_ref[...]).astype(jnp.bfloat16)
    resid_ref[...] = resid
    resid_f = resid.astype(jnp.float32)
    stats = jnp.sum(resid_f * resid_f, axis=1, keepdims=True) * (1.0 / width)
    gain = gain_ref[...].astype(jnp.float32).reshape(1, width)
    normed = (resid_f * lax.rsqrt(stats + 1e-05) * gain).astype(jnp.bfloat16)
    payload_ref[:, :width] = normed
    lane = lax.broadcasted_iota(jnp.int32, (rows, EXTRA), 1)
    routed = ((first == lane) | (second == lane)).astype(jnp.float32)
    payload_ref[:, width:] = routed.astype(jnp.bfloat16)


def own_offset(rows):
    return lax.axis_index("sub") * rows


def slot_matrix(extra, offset, block_rows, blocks, cap):
    count = extra.shape[0]
    here = lax.broadcasted_iota(jnp.int32, (count, count), 0)
    there = lax.broadcasted_iota(jnp.int32, (count, count), 1)
    before = (there // block_rows == here // block_rows) & ((there ^ offset) < (here ^ offset))
    earlier = dot(before.astype(jnp.bfloat16), extra)
    lane = lax.broadcasted_iota(jnp.int32, (count, EXTRA), 1)
    mine = lane == lax.axis_index("dev")
    rank = jnp.sum(jnp.where(mine, earlier, 0.0), axis=1, keepdims=True)
    routed = jnp.sum(jnp.where(mine, extra.astype(jnp.float32), 0.0), axis=1, keepdims=True)
    block = lax.broadcasted_iota(jnp.int32, (count, 1), 0) // block_rows
    base = jnp.zeros((count, 1), jnp.int32)
    for i, k in enumerate(blocks):
        base = jnp.where(block == i, k * cap, base)
    slot = jnp.where(routed > 0.5, rank.astype(jnp.int32) + base, -1)
    return (slot == lax.broadcasted_iota(jnp.int32, (count, EXTRA), 1)).astype(jnp.float32)


def hidden_columns(x, gate_ref, up_ref, out_ref, begin):
    step = min(512, out_ref.shape[1])
    end = out_ref.shape[1]
    for j in range(0, end, step):
        columns = slice(begin + j, begin + min(j + step, end))
        gate = dot(x, gate_ref[:, columns])
        up = dot(x, up_ref[:, columns])
        out_ref[:, j : min(j + step, end)] = (gate / (1.0 + jnp.exp(-gate)) * up).astype(jnp.bfloat16)


def join(piece_refs, rows_ref):
    at = 0
    for first, second in zip(piece_refs[0::2], piece_refs[1::2], strict=True):
        both = [first[...].astype(jnp.float32), second[...].astype(jnp.float32)]
        size = first.shape[0] + second.shape[0]
        rows_ref[at : at + size, :] = jnp.concatenate(both, axis=0).astype(jnp.bfloat16)
        at += size


def placed(rows_ref, width, piece_rows, blocks, cap, slots):
    block_rows = rows_ref.shape[0] // len(blocks)
    place = slot_matrix(rows_ref[:, width:], own_offset(piece_rows), block_rows, blocks, cap)
    return dot(place.T[:slots].astype(jnp.bfloat16), rows_ref[:, :width])


def pack_kernel(pieces, blocks, cap, *refs):
    x_ref, extra_ref, rows_ref = refs[pieces:]
    slots, width = x_ref.shape
    join(refs[:pieces], rows_ref)
    extra_ref[...] = rows_ref[:, width:]
    x_ref[...] = placed(rows_ref, width, refs[0].shape[0], blocks, cap, slots).astype(jnp.bfloat16)


def first_hidden_kernel(pieces, blocks, cap, *refs):
    packed_ref, gate_ref, up_ref, x_ref, extra_ref, hidden_ref, rows_ref = refs[pieces:]
    slots, width = x_ref.shape
    join(refs[:pieces], rows_ref)
    extra_ref[...] = rows_ref[:, width:]
    late = placed(rows_ref, width, refs[0].shape[0], blocks, cap, slots)
    x_ref[...] = (packed_ref[...].astype(jnp.float32) + late).astype(jnp.bfloat16)
    hidden_columns(x_ref[...], gate_ref, up_ref, hidden_ref, 0)


def next_hidden_kernel(begin, x_ref, gate_ref, up_ref, hidden_ref):
    hidden_columns(x_ref[...], gate_ref, up_ref, hidden_ref, begin)


def down_part(refs, sources, down_ref, own_width):
    sub = lax.axis_index("sub")
    total = None
    for which, start, width, bits, begin in sources:
        at = pl.multiple_of((sub ^ bits) * own_width + begin, 128)
        part = dot(refs[which][:, start : start + width], down_ref[pl.ds(at, width), :])
        total = part if total is None else total + part
    return total


def down_kernel(sources, own_width, has_total, *refs):
    rest = refs[-3:] if has_total else refs[-2:]
    total = down_part(refs, sources, rest[0], own_width)
    if has_total:
        total = total + rest[1][...]
    rest[-1][...] = total


def return_kernel(rows, order, cap, *refs):
    *extra_refs, x_ref, router_ref, spread_ref, share_ref = refs
    slots = share_ref.shape[0]
    extra = jnp.concatenate([ref[...] for ref in extra_refs], axis=0)
    here = slot_matrix(extra, own_offset(rows), extra.shape[0] // len(order), order, cap)
    spread_ref[...] = here.astype(jnp.bfloat16)
    routed = dot(here.T[:slots].astype(jnp.bfloat16), extra)[:, :EXPERTS] > 0.5
    logits = dot_nt(x_ref[...], router_ref[...])
    mine = lax.broadcasted_iota(jnp.int32, logits.shape, 1) == lax.axis_index("dev")
    own_logit = jnp.sum(jnp.where(mine, logits, 0.0), axis=1, keepdims=True)
    other_logit = jnp.sum(jnp.where(routed & ~mine, logits, 0.0), axis=1, keepdims=True)
    share = 1.0 / (1.0 + jnp.exp(other_logit - own_logit))
    share_ref[...] = jnp.broadcast_to(share, share_ref.shape)


def last_down_kernel(sources, operands, own_width, *refs):
    down_ref, total_ref, spread_ref, share_ref, *out_refs = refs[operands:]
    slots = total_ref.shape[0]
    total = total_ref[...] + down_part(refs, sources, down_ref, own_width)
    weighted = (total * share_ref[:, :1]).astype(jnp.bfloat16)
    result = dot(spread_ref[:, :slots], weighted).astype(jnp.bfloat16)
    height = out_refs[0].shape[0]
    for k, out_ref in enumerate(out_refs):
        out_ref[...] = result[k * height : (k + 1) * height]


def collect_kernel(rows, *refs):
    parts, (own_ref, *out_refs) = refs[:-4], refs[-4:]
    total = parts[0][...].astype(jnp.float32)
    for part in parts[1:]:
        total = total + part[...].astype(jnp.float32)
    own_ref[...] = total[:rows]
    for i, out_ref in enumerate(out_refs):
        out_ref[...] = total[(i + 1) * rows : (i + 2) * rows].astype(jnp.bfloat16)


def finish_kernel(resid_ref, *refs):
    *mixture_refs, out_ref = refs
    width = mixture_refs[0].shape[1]
    sub = lax.axis_index("sub")
    for bits, mixture_ref in enumerate(mixture_refs):
        lanes = pl.ds(pl.multiple_of((sub ^ bits) * width, 128), width)
        mixture = mixture_ref[...].astype(jnp.float32)
        out_ref[:, lanes] = (resid_ref[:, lanes].astype(jnp.float32) + mixture).astype(jnp.bfloat16)


def flip(x, axis, bits):
    return lax.ppermute(x, axis, [(i, i ^ bits) for i in range(lax.axis_size(axis))])


def per_device(
    tokens,
    queries,
    request_key_cache,
    request_value_cache,
    lengths,
    norm_gain,
    router_weight,
    routes,
    gate_weight,
    up_weight,
    down_weight,
):
    rows, width = tokens.shape
    devs, subs = lax.axis_size("dev"), lax.axis_size("sub")
    all_rows = rows * devs * subs
    cap = 5 * rows * subs // 6
    slots = devs * cap
    own_hidden = gate_weight.shape[1]
    out_width = down_weight.shape[1]
    bf16 = jnp.bfloat16
    opening = call(
        opening_kernel,
        jax.ShapeDtypeStruct((8, 128), jnp.float32),
        (),
        [],
        flops=OPENING_FLOPS,
        vmem=MIB,
    )
    operands = (
        opening,
        lengths,
        routes.T,
        queries,
        request_key_cache,
        request_value_cache,
        tokens,
        norm_gain,
    )
    payload, resid = call(
        attention_kernel,
        (
            jax.ShapeDtypeStruct((rows, width + EXTRA), bf16),
            jax.ShapeDtypeStruct((rows, width), bf16),
        ),
        operands,
        [VMEM_SPEC, SMEM_SPEC, SMEM_SPEC] + [VMEM_SPEC] * 5,
        flops=ATTENTION_FLOPS,
        bytes_accessed=100 * MIB,
        vmem=8 * MIB,
        scratch=[pltpu.VMEM((rows, width), jnp.float32)],
    )
    over_z = [payload] + [flip(payload, "dev", k) for k in range(1, devs)]
    over_x = [flip(p, "sub", 2) for p in over_z]
    pieces = [[z, flip(z, "sub", 1), x, flip(x, "sub", 1)] for z, x in zip(over_z, over_x, strict=True)]
    unit = own_hidden // 16
    widths = [unit * n for n in CHUNKS]
    begins = [sum(widths[:i]) for i in range(len(widths))]
    chunks = len(widths)
    early = [p for k in EARLY for p in pieces[k]]
    block_rows = all_rows // devs
    early_rows = block_rows * len(EARLY)
    packed, extra_early = call(
        functools.partial(pack_kernel, len(early), EARLY, cap),
        (
            jax.ShapeDtypeStruct((slots, width), bf16),
            jax.ShapeDtypeStruct((early_rows, EXTRA), bf16),
        ),
        early,
        [VMEM_SPEC] * len(early),
        flops=PACK_FLOPS,
        vmem=6 * MIB,
        scratch=[pltpu.VMEM((early_rows, width + EXTRA), bf16)],
    )
    late = [p for k in LATE for p in pieces[k]]
    late_rows = block_rows * len(LATE)
    x, extra_late, hidden = call(
        functools.partial(first_hidden_kernel, len(late), LATE, cap),
        (
            jax.ShapeDtypeStruct((slots, width), bf16),
            jax.ShapeDtypeStruct((late_rows, EXTRA), bf16),
            jax.ShapeDtypeStruct((slots, widths[0]), bf16),
        ),
        (*late, packed, gate_weight, up_weight),
        [VMEM_SPEC] * (len(late) + 3),
        flops=GATE_FLOPS,
        vmem=6 * MIB,
        scratch=[pltpu.VMEM((late_rows, width + EXTRA), bf16)],
    )
    own = [hidden]
    for i in range(1, chunks):
        own.append(
            call(
                functools.partial(next_hidden_kernel, begins[i]),
                jax.ShapeDtypeStruct((slots, widths[i]), bf16),
                (x, gate_weight, up_weight),
                [VMEM_SPEC] * 3,
                flops=GATE_FLOPS,
                vmem=4 * MIB,
            )
        )
    far = [flip(h, "sub", 2) for h in own]
    spread, share = call(
        functools.partial(return_kernel, rows, (*EARLY, *LATE), cap),
        (
            jax.ShapeDtypeStruct((all_rows, EXTRA), bf16),
            jax.ShapeDtypeStruct((slots, EXTRA), jnp.float32),
        ),
        (extra_early, extra_late, x, router_weight.T),
        [VMEM_SPEC] * 4,
        flops=DOWN_FLOPS,
        vmem=4 * MIB,
    )
    total_shape = jax.ShapeDtypeStruct((slots, out_width), jnp.float32)
    total = None
    for group in DOWN_GROUPS:
        taken, sources = [], []
        for i in group:
            for bits, array in ((2, far[i]), (1, flip(own[i], "sub", 1)), (3, flip(far[i], "sub", 1))):
                sources.append((len(taken), 0, widths[i], bits, begins[i]))
                taken.append(array)
            for n in [i] if i < chunks - 2 else [i, i + 1] if i == chunks - 2 else []:
                sources.append((len(taken), 0, widths[n], 0, begins[n]))
                taken.append(own[n])
        before = () if total is None else (total,)
        if group[-1] < chunks - 1:
            total = call(
                functools.partial(down_kernel, sources, own_hidden, total is not None),
                total_shape,
                (*taken, down_weight, *before),
                [VMEM_SPEC] * (len(taken) + 1 + len(before)),
                flops=DOWN_FLOPS * len(group),
                vmem=4 * MIB,
            )
        else:
            weighted = call(
                functools.partial(last_down_kernel, sources, len(taken), own_hidden),
                (jax.ShapeDtypeStruct((all_rows // devs, out_width), bf16),) * devs,
                (*taken, down_weight, total, spread, share),
                [VMEM_SPEC] * (len(taken) + 4),
                flops=DOWN_FLOPS,
                vmem=4 * MIB,
            )
    weighted = dict(zip((*EARLY, *LATE), weighted, strict=True))
    arrived = [weighted[0]] + [flip(weighted[k], "dev", k) for k in Z_ORDER]
    mixed, to_near, to_far, to_across = call(
        functools.partial(collect_kernel, rows),
        (jax.ShapeDtypeStruct((rows, out_width), jnp.float32),)
        + (jax.ShapeDtypeStruct((rows, out_width), bf16),) * 3,
        arrived,
        [VMEM_SPEC] * devs,
        flops=10**6,
        vmem=4 * MIB,
    )
    from_near = flip(to_near, "sub", 1)
    from_far = flip(to_far, "sub", 2)
    from_across = flip(to_across, "sub", 3)
    return call(
        finish_kernel,
        jax.ShapeDtypeStruct((rows, width), bf16),
        (resid, mixed, from_near, from_far, from_across),
        [VMEM_SPEC] * 5,
        flops=10**6,
        vmem=4 * MIB,
    )


def solution(mesh):
    in_specs = (
        P(("rep", "dev", "sub"), None),
        P(("rep", "dev", "sub"), None),
        P(("rep", "dev", "sub"), None, None),
        P(("rep", "dev", "sub"), None, None),
        P(("rep", "dev", "sub")),
        P(),
        P(),
        P(("rep", "dev"), None),
        P(None, ("dev", "sub")),
        P(None, ("dev", "sub")),
        P("dev", "sub"),
    )
    out_specs = P(("rep", "dev", "sub"), None)
    one_expert_each = mesh.shape["dev"] == EXPERTS and mesh.shape["sub"] == 4
    return jax.shard_map(
        per_device if one_expert_each else general_plan,
        mesh=mesh,
        in_specs=in_specs,
        out_specs=out_specs,
        check_vma=False,
    )
```
